256 devices in a mesh: gx: 16 (over y, x), gy: 16 (over z, core).
Axes of the slice: x: 4, y: 4, z: 8, core: 2. Of those that a mesh axis runs over, the one named last changes fastest.
Arguments:
- pressure: float32 [2, 2048, 2048], P(None, 'gx', 'gy'), may hold values from 0.5 to 1.5
- saturations: float32 [2, 2, 2048, 2048], P(None, None, 'gx', 'gy'), may hold values from 0.05 to 0.4
- old_mass: float32 [3, 2, 2048, 2048], P(None, None, 'gx', 'gy'), may hold values from 0 to 0.4
- pore_volume: float32 [2, 2048, 2048], P(None, 'gx', 'gy'), may hold values from 0.3 to 3
- transmissibility: float32 [3, 2, 2048, 2048], P(None, None, 'gx', 'gy'), may hold values from 0.3 to 3
- direction: float32 [3, 2, 2048, 2048], P(None, None, 'gx', 'gy'), may hold values from -6 to 6
- seg_pressure: float32 [512, 128], P('gx'), may hold values from 0.4 to 1.2
- seg_direction: float32 [512, 128], P('gx'), may hold values from -6 to 6
- perf_cell: int32 [512, 128], P('gx'), may hold values from 0 to 524287, as said below
- well_index: float32 [512, 128], P('gx'), may hold values from 0.2 to 2
- parent: int32 [512, 128], P('gx'), may hold values from 0 to 126, as said below
- seg_head: float32 [512, 128], P('gx'), may hold values from 0 to 0.3
- well_mode: int32 [512], P('gx'), may hold values from 0 to 1
- bhp_limit: float32 [512], P('gx'), may hold values from 0.3 to 0.8
- guide_rate: float32 [512], P('gx'), may hold values from 0.5 to 5
- group_of: int32 [512, 1], P('gx'), may hold values from 0 to 127
- group_target: float32 [128], replicated, may hold values from 200 to 800
Outputs:
- cell_residual: float32 [3, 2, 2048, 2048], P(None, None, 'gx', 'gy')
- cell_jvp: float32 [3, 2, 2048, 2048], P(None, None, 'gx', 'gy')
- seg_residual: float32 [512, 128], P(('gx', 'gy'))
- seg_jvp: float32 [512, 128], P(('gx', 'gy'))
- group_rates: float32 [3, 128], replicated
The draws below stay inside these ranges and needn't reach their ends.
Inputs may be any that keep to these rules, and one draw needn't show every extreme that they name: perf_cell codes (layer * 128 + xl) * 2048 + row, with xl the column within the strip of 128 columns of the well's block of 32 wells. `parent`: segment 0 of every well names itself; every other segment names a segment of lower number. `group_of`: every group has at least one well.
All inputs are finite; a program needn't handle non-finite values.
Results may differ from the reference program's by a relative error of at most 0.0003.
Values sent between devices are 32-bit elements; how exact they have to be, the bound alone decides.
A program may use at most 128 MiB of HBM per device.

```python
import math
import jax
import jax.numpy as jnp
from jax import lax

NZ = 2
CX = 128
WELL_GX = 32
SEG = 128
GROUPS = 128
NX = 2048
NY = 2048
WELLS = 512


def draw_perf_cell(key, part):
    keys = jax.random.split(jax.random.fold_in(key, 11), 5)
    head_col = jax.random.randint(keys[0], (WELLS, 1), 0, CX)
    head_row = jax.random.randint(keys[1], (WELLS, 1), 0, NY)
    column = jnp.clip(head_col + jax.random.randint(keys[2], (WELLS, SEG), -2, 3), 0, CX - 1)
    row_pos = jnp.clip(head_row + jax.random.randint(keys[3], (WELLS, SEG), -8, 9), 0, NY - 1)
    layer = jax.random.randint(keys[4], (WELLS, SEG), 0, NZ)
    coded = ((layer * CX + column) * NY + row_pos).astype(jnp.int32)
    coded = coded.at[WELLS - 1, SEG - 1].set(NZ * CX * NY - 1)
    coded = coded.at[0, 0].set(0)
    return coded


def draw_parent(key, part):
    upper = jnp.maximum(jnp.arange(SEG, dtype=jnp.int32), 1)
    chosen = jax.random.randint(jax.random.fold_in(key, 23), (WELLS, SEG), 0, upper[None, :])
    chosen = chosen.at[:, SEG - 1].set(SEG - 2)
    return chosen.astype(jnp.int32)


def place_ends(drawn, stream_key, least, largest):
    extent = drawn.shape
    place = [jax.random.randint(jax.random.fold_in(stream_key, axis), (), 0, extent[axis]) for axis in range(len(extent))]
    drawn = drawn.at[tuple(place)].set(least)
    longest = extent.index(max(extent))
    place[longest] = (place[longest] + 1) % extent[longest]
    return drawn.at[tuple(place)].set(largest)


def levels(own_key, shape, cuts, smallest, high):
    loudness, own = 1.0, jax.random.fold_in(own_key, 6)
    for dim, shards_of in cuts:
        steps = jnp.exp(jax.random.uniform(jax.random.fold_in(own, dim), (shards_of,), jnp.float32, smallest / len(cuts), high / len(cuts)))
        loudness = loudness * jnp.repeat(steps, shape[dim] // shards_of).reshape([-1 if axis == dim else 1 for axis in range(len(shape))])
    return loudness


def picks_of(rng, rows, amount, top, lift):
    order = jax.random.permutation(jax.random.fold_in(rng, 1), amount)
    favour = order
    for power in range(3):
        favour = favour * favour // amount
    favour = favour * lift // amount
    chance = jax.random.randint(jax.random.fold_in(rng, 2), (rows, amount), 0, 4096) + favour
    holders = jax.random.permutation(jax.random.fold_in(rng, 3), rows)[jnp.arange(amount) % rows]
    chance = jnp.where(jnp.arange(rows)[:, None] == holders[None, :], 1 << 14, chance)
    priority = chance * amount + jnp.arange(amount)
    return lax.top_k(priority.astype(jnp.int32), top)[1].astype(jnp.int32)


def bell_draw(key, shape, spread, limit, cuts=(), held_as=jnp.bfloat16):
    loudness = levels(key, shape, cuts, -0.22, 0.18) if cuts else 1.0
    drawn = jax.random.normal(key, shape, jnp.float32) * spread * loudness
    return jnp.minimum(jnp.maximum(drawn, -limit), limit).astype(held_as)


def setup_inputs(seed: int = 0) -> dict:
    splits = jax.random.split(jax.random.key(seed), 18)
    pressure = jnp.clip(0.5 + 1.0 * jax.random.uniform(splits[0], (NZ, NX, NY), jnp.float32) ** levels(splits[0], (NZ, NX, NY), ((1, 16), (2, 16)), -0.2, 0.2), 0.5, 1.5)
    saturations = jnp.clip(0.05 + 0.35 * jax.random.uniform(splits[1], (2, NZ, NX, NY), jnp.float32) ** levels(splits[1], (2, NZ, NX, NY), ((2, 16), (3, 16)), -0.2, 0.2), 0.05, 0.4)
    old_mass = jnp.clip(0.4 * jax.random.uniform(splits[2], (3, NZ, NX, NY), jnp.float32) ** levels(splits[2], (3, NZ, NX, NY), ((2, 16), (3, 16)), -0.2, 0.2), 0.0, 0.4)
    pore_volume = jnp.clip(jnp.exp(math.log(3.0) - 2.3025851 * jax.random.uniform(splits[3], (NZ, NX, NY), jnp.float32) ** levels(splits[3], (NZ, NX, NY), ((1, 16), (2, 16)), -0.2, 0.2)), 0.3, 3.0)
    transmissibility = jnp.clip(jnp.exp(math.log(3.0) - 2.3025851 * jax.random.uniform(splits[4], (3, NZ, NX, NY), jnp.float32) ** levels(splits[4], (3, NZ, NX, NY), ((2, 16), (3, 16)), -0.2, 0.2)), 0.3, 3.0)
    direction = bell_draw(splits[5], (3, NZ, NX, NY), 1.0, 6.0, ((2, 16), (3, 16)), jnp.float32)
    seg_pressure = jnp.clip(0.4 + 0.800000042 * jax.random.uniform(splits[6], (WELLS, SEG), jnp.float32) ** levels(splits[6], (WELLS, SEG), ((0, 16),), -0.2, 0.2), 0.4, 1.2)
    seg_direction = bell_draw(splits[7], (WELLS, SEG), 1.0, 6.0, ((0, 16),), jnp.float32)
    perf_cell = draw_perf_cell(jax.random.fold_in(splits[17], 71), 0)
    well_index = jnp.clip(jnp.exp(math.log(2.0) - 2.3025851 * jax.random.uniform(splits[9], (WELLS, SEG), jnp.float32) ** levels(splits[9], (WELLS, SEG), ((0, 16),), -0.2, 0.2)), 0.2, 2.0)
    parent = draw_parent(jax.random.fold_in(splits[17], 71), 0)
    seg_head = jnp.clip(0.3 * jax.random.uniform(splits[11], (WELLS, SEG), jnp.float32) ** levels(splits[11], (WELLS, SEG), ((0, 16),), -0.2, 0.2), 0.0, 0.3)
    well_mode = place_ends(jax.random.randint(splits[12], (WELLS,), 0, 2), jax.random.fold_in(splits[12], 1), 0, 1).astype(jnp.int32)
    bhp_limit = jnp.clip(0.3 + 0.5 * jax.random.uniform(splits[13], (WELLS,), jnp.float32) ** levels(splits[13], (WELLS,), ((0, 16),), -0.2, 0.2), 0.3, 0.8)
    guide_rate = jnp.clip(jnp.exp(math.log(5.0) - 2.3025851 * jax.random.uniform(splits[14], (WELLS,), jnp.float32) ** levels(splits[14], (WELLS,), ((0, 16),), -0.2, 0.2)), 0.5, 5.0)
    group_of = picks_of(splits[15], WELLS, GROUPS, 1, 64)
    group_target = jnp.clip(jax.random.uniform(splits[16], (GROUPS,), jnp.float32, 200.0, 800.0), 200.0, 800.0)
    return {"pressure": pressure, "saturations": saturations, "old_mass": old_mass, "pore_volume": pore_volume, "transmissibility": transmissibility, "direction": direction, "seg_pressure": seg_pressure, "seg_direction": seg_direction, "perf_cell": perf_cell, "well_index": well_index, "parent": parent, "seg_head": seg_head, "well_mode": well_mode, "bhp_limit": bhp_limit, "guide_rate": guide_rate, "group_of": group_of, "group_target": group_target}


COMPRESS = (0.05, 0.2, 1.0)
VISCOSITY = (0.5, 1.0, 0.2)
DENSITY = (1.0, 0.8, 0.2)
ROCK_COMP = 0.01
GRAVITY = 0.05
UPWIND_WIDTH = 0.02
FRICTION = 0.002
RATE_SCALE = 0.1


def phase_props(press, water, gas):
    oil = 1.0 - water - gas
    satur = (water, oil, gas)
    rock = 1.0 + ROCK_COMP * (press - 1.0)
    mobility = []
    masses = []
    for phase in range(3):
        volume = jnp.exp(COMPRESS[phase] * (press - 1.0))
        mobility.append(satur[phase] * satur[phase] * volume / VISCOSITY[phase])
        masses.append(rock * satur[phase] * volume)
    return jnp.stack(mobility), jnp.stack(masses)


def face_flux(press_in, press_out, mobil_in, mobil_out, trans, lift):
    fluxes = []
    for phase in range(3):
        potential = press_in - press_out + DENSITY[phase] * lift
        upwind = jax.nn.sigmoid(potential / UPWIND_WIDTH)
        fluxes.append(trans * (upwind * mobil_in[phase] + (1.0 - upwind) * mobil_out[phase]) * potential)
    return jnp.stack(fluxes)


def ancestry(parent):
    count = parent.shape[1]
    segment_ids = jnp.arange(count, dtype=jnp.int32)
    reach = (segment_ids[None, :, None] == segment_ids[None, None, :]) | (parent[:, None, :] == segment_ids[None, :, None])
    reach = reach.astype(jnp.float32)
    for level in range((count - 1).bit_length()):
        reach = jnp.minimum(jnp.einsum("wsu,wut->wst", reach, reach, precision=lax.Precision.HIGHEST), 1.0)
    return reach


def reference(pressure, saturations, old_mass, pore_volume, transmissibility, direction, seg_pressure, seg_direction, perf_cell, well_index, parent, seg_head, well_mode, bhp_limit, guide_rate, group_of, group_target):
    layer_span = CX * NY
    layer = perf_cell // layer_span
    remain = perf_cell % layer_span
    column = (jnp.arange(WELLS, dtype=jnp.int32) // WELL_GX)[:, None] * CX + remain // NY
    flat_cell = ((layer * NX + column) * NY + remain % NY).astype(jnp.int32)
    reach = ancestry(parent)
    member = (group_of[:, 0][:, None] == jnp.arange(GROUPS, dtype=jnp.int32)[None, :]).astype(jnp.float32)
    guide_total = jnp.dot(guide_rate, member, precision=lax.Precision.HIGHEST)
    target = jnp.dot(member, group_target, precision=lax.Precision.HIGHEST) * guide_rate / jnp.dot(member, guide_total, precision=lax.Precision.HIGHEST)

    def evaluate(press, satur, seg_press):
        mobility, masses = phase_props(press, satur[0], satur[1])
        residual = masses * pore_volume - old_mass
        flux_cols = face_flux(press[:, :-1], press[:, 1:], mobility[:, :, :-1], mobility[:, :, 1:], transmissibility[0][:, :-1], 0.0)
        residual = residual + jnp.pad(flux_cols, ((0, 0), (0, 0), (0, 1), (0, 0))) - jnp.pad(flux_cols, ((0, 0), (0, 0), (1, 0), (0, 0)))
        flux_rows = face_flux(press[:, :, :-1], press[:, :, 1:], mobility[:, :, :, :-1], mobility[:, :, :, 1:], transmissibility[1][:, :, :-1], 0.0)
        residual = residual + jnp.pad(flux_rows, ((0, 0), (0, 0), (0, 0), (0, 1))) - jnp.pad(flux_rows, ((0, 0), (0, 0), (0, 0), (1, 0)))
        flux_layers = face_flux(press[:-1], press[1:], mobility[:, :-1], mobility[:, 1:], transmissibility[2][:-1], GRAVITY)
        residual = residual + jnp.pad(flux_layers, ((0, 0), (0, 1), (0, 0), (0, 0))) - jnp.pad(flux_layers, ((0, 0), (1, 0), (0, 0), (0, 0)))
        mobil_flat = mobility.reshape(3, -1)
        rates = well_index * mobil_flat[:, flat_cell] * (press.reshape(-1)[flat_cell] - seg_press)
        residual = residual.reshape(3, -1).at[:, flat_cell.reshape(-1)].add(rates.reshape(3, -1)).reshape(residual.shape)
        flow = jnp.einsum("wst,wt->ws", reach, jnp.sum(rates, axis=0), precision=lax.Precision.HIGHEST)
        above = jnp.take_along_axis(seg_press, parent, axis=1)
        inner = seg_press - above - seg_head - FRICTION * flow
        root = jnp.where(well_mode == 1, RATE_SCALE * (flow[:, 0] - target), seg_press[:, 0] - bhp_limit)
        seg_res = inner.at[:, 0].set(root)
        return residual, seg_res, rates

    primal, tangent = jax.jvp(evaluate, (pressure, saturations, seg_pressure), (direction[0], direction[1:], seg_direction))
    cell_residual, seg_residual, rates = primal
    cell_jvp, seg_jvp, unused_rates = tangent
    group_rates = jnp.dot(jnp.sum(rates, axis=2), member, precision=lax.Precision.HIGHEST)
    return cell_residual, cell_jvp, seg_residual, seg_jvp, group_rates
```

```python
import jax
import jax.numpy as jnp
from jax import lax
from jax.experimental import pallas as pl
from jax.experimental.pallas import tpu as pltpu
from jax.sharding import PartitionSpec as P

COMPRESS = (0.05, 0.2, 1.0)
VISCOSITY = (0.5, 1.0, 0.2)
DENSITY = (1.0, 0.8, 0.2)
ROCK_COMP = 0.01
GRAVITY = 0.05
UPWIND_WIDTH = 0.02
FRICTION = 0.002
RATE_SCALE = 0.1

MESH = pl.DeviceIdType.MESH
F32 = jnp.float32
BF16 = jnp.bfloat16
NT = (((1,), (1,)), ((), ()))

CH = 32
WELLS_SCATTER = 8


def iota(shape, dim):
    return lax.broadcasted_iota(jnp.int32, shape, dim)


def split2(x):
    high = x.astype(BF16).astype(F32)
    return high, x - high


def split3(x):
    high = x.astype(BF16).astype(F32)
    rest = x - high
    mid = rest.astype(BF16).astype(F32)
    return high, mid, rest - mid


def mobilities(press, water, gas, dpress, dwater, dgas):
    satur = (water, 1.0 - water - gas, gas)
    dsatur = (dwater, -dwater - dgas, dgas)
    volumes, mobil, dmobil = [], [], []
    for a in range(3):
        volume = jnp.exp(COMPRESS[a] * (press - 1.0))
        scaled = satur[a] * volume * (1.0 / VISCOSITY[a])
        volumes.append(volume)
        mobil.append(satur[a] * scaled)
        dmobil.append(scaled * (2.0 * dsatur[a] + COMPRESS[a] * satur[a] * dpress))
    return satur, dsatur, volumes, mobil, dmobil


def upwinding(potential, dpotential):
    half = jnp.tanh(potential * (0.5 / UPWIND_WIDTH))
    upwind = 0.5 + 0.5 * half
    dupwind = (1.0 - half * half) * (0.25 / UPWIND_WIDTH) * dpotential
    return upwind, dupwind


def face(trans, pot, dpot, up, dup, m_in, m_out, dm_in, dm_out):
    jump = m_in - m_out
    mean = m_out + up * jump
    dmean = dm_out + up * (dm_in - dm_out) + dup * jump
    flow = trans * pot
    return flow * mean, flow * dmean + (trans * dpot) * mean


def kernel(
    nx, ny, n_well,
    press, sat, old, pore, trans, direc, seg_p, seg_d, perf, windex, parent, head,
    mode, bhp, guide, group, gtarget,
    res, jvp, seg_res, seg_jvp, grates,
    mhl, gath, rates, mob, colf, edge, halo_tx, halo_rx, msg, rx1, msg2, rx2,
    s_h, r_h, s_1, r_1, s_2, r_2,
):
    cx, cy = press.shape[1], press.shape[2]
    gx, gy = lax.axis_index("gx"), lax.axis_index("gy")
    share = n_well // ny
    state = lambda q, l: (press[l], sat[0, l], sat[1, l], direc[0, l], direc[1, l], direc[2, l])[q]

    barrier = pltpu.get_barrier_semaphore()
    for k in range(1, ny):
        pl.semaphore_signal(barrier, inc=1, device_id={"gy": lax.rem(gy + k, ny)}, device_id_type=MESH)
    for k in range(1, nx):
        pl.semaphore_signal(barrier, inc=1, device_id={"gx": lax.rem(gx + k, nx)}, device_id_type=MESH)

    lane = iota((cx, cy), 1)
    acc = jnp.zeros((cx, cy), F32)
    for l in range(2):
        for q in range(7):
            block = trans.at[0, l] if q == 6 else None
            if q < 6:
                block = (press.at[l], sat.at[0, l], sat.at[1, l], direc.at[0, l], direc.at[1, l], direc.at[2, l])[q]
            row = 2 * q + l
            halo_tx[0, row:row + 1, :] = block[cx - 1:cx, :]
            halo_tx[1, row:row + 1, :] = block[0:1, :]
            lanes = trans[1, l] if q == 6 else block[...]
            acc = jnp.where(lane == row, lanes[:, cy - 1:cy], acc)
            acc = jnp.where(lane == 16 + row, lanes[:, 0:1], acc)
            if q < 6:
                high, low = split2(lanes)
                at = (q * 2 + l) * cx
                mhl[at:at + cx, 0:cy] = high.astype(BF16)
                mhl[at:at + cx, cy:2 * cy] = low.astype(BF16)
    flipped = acc.T
    halo_tx[2] = flipped[0:16]
    halo_tx[3] = flipped[16:32]
    halo_tx[0, 14:16, :] = jnp.zeros((2, cy), F32)
    halo_tx[1, 14:16, :] = jnp.zeros((2, cy), F32)

    pl.semaphore_wait(barrier, nx + ny - 2)

    copies = []

    def send(src, dst, s_sem, r_sem, where):
        copy = pltpu.make_async_remote_copy(
            src_ref=src, dst_ref=dst, send_sem=s_sem, recv_sem=r_sem, device_id=where, device_id_type=MESH
        )
        copy.start()
        return copy

    targets = (
        {"gx": lax.rem(gx + 1, nx)},
        {"gx": lax.rem(gx + nx - 1, nx)},
        {"gy": lax.rem(gy + 1, ny)},
        {"gy": lax.rem(gy + ny - 1, ny)},
    )
    halo = [send(halo_tx.at[f], halo_rx.at[f], s_h.at[f], r_h.at[f], targets[f]) for f in range(4)]

    all_rows = cy * ny
    shift = all_rows.bit_length() - 1
    first_row = gy * cy

    def split_cell(cell):
        return lax.shift_right_logical(cell, shift), (cell & (all_rows - 1)) - first_row

    def gather(c, _):
        w = 2 * c
        cell = jnp.concatenate([perf[pl.ds(w, 1), :], perf[pl.ds(w + 1, 1), :]], axis=1)
        col, row = split_cell(cell)
        hot = (iota((cy, cell.shape[1]), 0) == row).astype(F32).astype(BF16)
        hot = jnp.concatenate([hot, hot], axis=0)
        pick = iota((2 * cx, cell.shape[1]), 0) == col
        for q in range(6):
            got = jnp.dot(mhl[q * 2 * cx:(q + 1) * 2 * cx, :], hot, preferred_element_type=F32)
            got = jnp.sum(jnp.where(pick, got, 0.0), axis=0, keepdims=True)
            half = cell.shape[1] // 2
            gath[q, pl.ds(w, 1), :] = got[:, :half]
            gath[q, pl.ds(w + 1, 1), :] = got[:, half:]
        return 0

    lax.fori_loop(0, n_well // 2, gather, 0)

    col, row = split_cell(perf[...])
    weight = jnp.where((row >= 0) & (row < cy), windex[...], 0.0)
    values = [gath[q] for q in range(6)]
    _, _, _, m, dm = mobilities(*values)
    drop = weight * (values[0] - seg_p[...])
    ddrop = weight * (values[3] - seg_d[...])
    well = iota((n_well, n_well), 0) == iota((n_well, n_well), 1)
    group_col = jnp.sum(jnp.where(well, group[...].astype(F32), 0.0), axis=1, keepdims=True)
    guide_col = jnp.sum(jnp.where(well, guide[...], 0.0), axis=1, keepdims=True)
    groups = gtarget.shape[1]
    member = group_col == iota((n_well, groups), 1).astype(F32)
    guide_part = jnp.sum(jnp.where(member, guide_col, 0.0), axis=0, keepdims=True)
    total = jnp.zeros_like(drop)
    dtotal = jnp.zeros_like(drop)
    parts = []
    for a in range(3):
        rate = m[a] * drop
        drate = dm[a] * drop + m[a] * ddrop
        rates[a] = rate
        rates[3 + a] = drate
        total = total + rate
        dtotal = dtotal + drate
        by_well = jnp.sum(rate, axis=1, keepdims=True)
        parts.append(jnp.sum(jnp.where(member, by_well, 0.0), axis=0, keepdims=True))
    tail = jnp.concatenate(parts + [jnp.zeros_like(parts[0])], axis=0)
    for d in range(ny):
        msg[d, 0:2, :] = total[2 * d:2 * d + 2]
        msg[d, 2:4, :] = dtotal[2 * d:2 * d + 2]
        msg[d, 4:8, :] = tail
    first = []
    for k in range(1, ny):
        to = lax.rem(gy + k, ny)
        first.append(send(msg.at[to], rx1.at[k], s_1.at[k], r_1.at[k], {"gy": to}))

    last = (iota((CH, cy), 1) == cy - 1)
    for l in range(2):
        for q in range(8):
            mob[q, l, cx:cx + 8, :] = jnp.zeros((8, cy), F32)
    colf[:, :, 0:8, :] = jnp.zeros((6, 2, 8, cy), F32)
    for c in range(cx // CH):
        at = slice(c * CH, (c + 1) * CH)
        props = []
        for l in range(2):
            v = (press[l, at], sat[0, l, at], sat[1, l, at], direc[0, l, at], direc[1, l, at], direc[2, l, at])
            satur, dsatur, volume, m, dm = mobilities(*v)
            rock = (1.0 + ROCK_COMP * (v[0] - 1.0)) * pore[l, at]
            drock = ROCK_COMP * v[3] * pore[l, at]
            mob[6, l, at, :] = v[0]
            mob[7, l, at, :] = v[3]
            pot = v[0] - pltpu.roll(v[0], cy - 1, 1)
            dpot = v[3] - pltpu.roll(v[3], cy - 1, 1)
            t = jnp.where(last, 0.0, trans[1, l, at])
            up, dup = upwinding(pot, dpot)
            for a in range(3):
                mob[a, l, at, :] = m[a]
                mob[3 + a, l, at, :] = dm[a]
                mass = satur[a] * volume[a]
                dmass = (dsatur[a] + COMPRESS[a] * satur[a] * v[3]) * volume[a]
                f, df = face(
                    t, pot, dpot, up, dup, m[a], pltpu.roll(m[a], cy - 1, 1), dm[a], pltpu.roll(dm[a], cy - 1, 1)
                )
                res[a, l, at, :] = rock * mass - old[a, l, at] + (f - pltpu.roll(f, 1, 1))
                jvp[a, l, at, :] = drock * mass + rock * dmass + (df - pltpu.roll(df, 1, 1))
            props.append((v[0], v[3], m, dm))
        (p0, d0, m0, dm0), (p1, d1, m1, dm1) = props
        t = trans[2, 0, at]
        for a in range(3):
            pot = p0 - p1 + DENSITY[a] * GRAVITY
            dpot = d0 - d1
            up, dup = upwinding(pot, dpot)
            f, df = face(t, pot, dpot, up, dup, m0[a], m1[a], dm0[a], dm1[a])
            res[a, 0, at, :] += f
            jvp[a, 0, at, :] += df
            res[a, 1, at, :] -= f
            jvp[a, 1, at, :] -= df

    sums = msg[gy]
    for k in range(1, ny):
        first[k - 1].wait_recv()
        sums = sums + rx1[k]
    msg2[0:3, :] = sums[4:7]
    msg2[3:4, :] = guide_part
    msg2[4:8, :] = jnp.zeros((4, groups), F32)
    second = []
    for k in range(1, nx):
        second.append(send(msg2, rx2.at[k], s_2.at[k], r_2.at[k], {"gx": lax.rem(gx + k, nx)}))

    for l in range(2):
        for c in range(cx // CH):
            at = slice(c * CH, (c + 1) * CH)
            nxt = slice(c * CH + 1, (c + 1) * CH + 1)
            here = slice(c * CH + 8, (c + 1) * CH + 8)
            t = trans[0, l, at]
            if c == cx // CH - 1:
                t = jnp.where(iota((CH, cy), 0) == CH - 1, 0.0, t)
            pot = mob[6, l, at] - mob[6, l, nxt]
            dpot = mob[7, l, at] - mob[7, l, nxt]
            up, dup = upwinding(pot, dpot)
            for a in range(3):
                f, df = face(
                    t, pot, dpot, up, dup, mob[a, l, at], mob[a, l, nxt], mob[3 + a, l, at], mob[3 + a, l, nxt]
                )
                colf[a, l, here, :] = f
                colf[3 + a, l, here, :] = df
        for c in range(cx // CH):
            at = slice(c * CH, (c + 1) * CH)
            here = slice(c * CH + 8, (c + 1) * CH + 8)
            prev = slice(c * CH + 7, (c + 1) * CH + 7)
            for a in range(3):
                res[a, l, at, :] += colf[a, l, here] - colf[a, l, prev]
                jvp[a, l, at, :] += colf[3 + a, l, here] - colf[3 + a, l, prev]

    def scatter(c, _):
        hots, sides = [], [[] for _ in range(6)]
        for i in range(WELLS_SCATTER):
            w = c * WELLS_SCATTER + i
            col, row = split_cell(perf[pl.ds(w, 1), :])
            n = col.shape[1]
            hot = (iota((2 * cx, n), 0) == col).astype(F32).astype(BF16)
            hots += [hot, hot]
            hit = (iota((cy, n), 0) == row).astype(F32).astype(BF16).reshape(cy // 16, 16, n)
            for q in range(6):
                for part in split2(rates[q, pl.ds(w, 1), :]):
                    wide = jnp.broadcast_to(part, (16, n)).astype(BF16)
                    sides[q].append((hit * wide[None]).reshape(cy, n))
        hot = jnp.concatenate(hots, axis=1)
        for a in range(3):
            side = jnp.concatenate(
                [jnp.concatenate(sides[a], axis=1), jnp.concatenate(sides[3 + a], axis=1)], axis=0
            )
            out = lax.dot_general(hot, side, NT, preferred_element_type=F32)
            for l in range(2):
                res[a, l] += out[l * cx:(l + 1) * cx, :cy]
                jvp[a, l] += out[l * cx:(l + 1) * cx, cy:]
        return 0

    lax.fori_loop(0, n_well // WELLS_SCATTER, scatter, 0)

    n_seg = perf.shape[1]
    flows, aboves, owns = [], [], []
    for i in range(share):
        w = gy * share + i
        up_of = parent[pl.ds(w, 1), :]
        down = iota((n_seg, n_seg), 0)
        link = down == up_of
        reach = jnp.where(link | (down == iota((n_seg, n_seg), 1)), 1.0, 0.0).astype(BF16)
        for _ in range((n_seg - 1).bit_length()):
            square = jnp.dot(reach, reach, preferred_element_type=F32)
            reach = jnp.minimum(square, 1.0).astype(BF16)
        vals = split3(sums[i:i + 1]) + split3(sums[2 + i:3 + i])
        vals = jnp.concatenate(vals + (jnp.zeros((2, n_seg), F32),), axis=0).astype(BF16)
        flow = lax.dot_general(vals, reach, NT, preferred_element_type=F32)
        own = (seg_p[pl.ds(w, 1), :], seg_d[pl.ds(w, 1), :])
        vals = split3(own[0]) + split3(own[1])
        vals = jnp.concatenate(vals + (jnp.zeros((2, n_seg), F32),), axis=0).astype(BF16)
        above = jnp.dot(vals, jnp.where(link, 1.0, 0.0).astype(BF16), preferred_element_type=F32)
        flows.append((flow[0:1] + flow[1:2] + flow[2:3], flow[3:4] + flow[4:5] + flow[5:6]))
        aboves.append((above[0:1] + above[1:2] + above[2:3], above[3:4] + above[4:5] + above[5:6]))
        owns.append(own)

    for f in range(4):
        halo[f].wait_recv()
    ins, outs = [], []
    for q in range(7):
        r = slice(2 * q, 2 * q + 2)
        ins.append(jnp.concatenate([halo_rx[0, r], halo_tx[0, r], halo_rx[2, r], halo_tx[2, r]], axis=0))
        outs.append(jnp.concatenate([halo_tx[1, r], halo_rx[1, r], halo_tx[3, r], halo_rx[3, r]], axis=0))
    side = iota((8, cy), 0) // 2
    outer = (
        ((side == 0) & (gx == 0)) | ((side == 1) & (gx == nx - 1))
        | ((side == 2) & (gy == 0)) | ((side == 3) & (gy == ny - 1))
    )
    t = jnp.where(outer, 0.0, ins[6])
    pot, dpot = ins[0] - outs[0], ins[3] - outs[3]
    up, dup = upwinding(pot, dpot)
    m_in, m_out = mobilities(*ins[:6]), mobilities(*outs[:6])
    faces = [
        face(t, pot, dpot, up, dup, m_in[3][a], m_out[3][a], m_in[4][a], m_out[4][a]) for a in range(3)
    ]
    edge[...] = jnp.zeros((cx, cy), F32)
    for a in range(3):
        for o, out in enumerate((res, jvp)):
            for l in range(2):
                out[a, l, 0:1, :] -= faces[a][o][l:l + 1]
                out[a, l, cx - 1:cx, :] += faces[a][o][2 + l:3 + l]
            edge[(2 * a + o) * 4:(2 * a + o) * 4 + 4, :] = faces[a][o][4:8]
    turned = edge[...].T
    for a in range(3):
        for o, out in enumerate((res, jvp)):
            for l in range(2):
                at = (2 * a + o) * 4 + l
                delta = jnp.where(lane == 0, -turned[:, at:at + 1], 0.0)
                out[a, l] += jnp.where(lane == cy - 1, turned[:, at + 2:at + 3], delta)

    everything = msg2[...]
    for k in range(1, nx):
        second[k - 1].wait_recv()
        everything = everything + rx2[k]
    grates[...] = everything[0:3]
    guide_total = everything[3:4]

    wells = iota((1, n_well), 1)
    segs = iota((1, n_seg), 1)
    names = iota((1, groups), 1).astype(F32)
    for i in range(share):
        w = gy * share + i
        mine = wells == w
        pick = lambda ref: jnp.sum(jnp.where(mine, ref[...].astype(F32), 0.0), axis=1, keepdims=True)
        chosen = names == pick(group)
        named = lambda row: jnp.sum(jnp.where(chosen, row, 0.0), axis=1, keepdims=True)
        target = named(gtarget[...]) * pick(guide) / named(guide_total)
        rated = pick(mode) == 1.0
        (flow, dflow), (above, dabove), (own, down) = flows[i], aboves[i], owns[i]
        inner = own - above - head[pl.ds(w, 1), :] - FRICTION * flow
        root = jnp.where(rated, RATE_SCALE * (flow - target), own - pick(bhp))
        seg_res[i:i + 1, :] = jnp.where(segs == 0, root, inner)
        inner = down - dabove - FRICTION * dflow
        root = jnp.where(rated, RATE_SCALE * dflow, down)
        seg_jvp[i:i + 1, :] = jnp.where(segs == 0, root, inner)

    for copy in halo + first + second:
        copy.wait_send()


def solution(mesh):
    nx, ny = mesh.shape["gx"], mesh.shape["gy"]

    def per_device(
        pressure, saturations, old_mass, pore_volume, transmissibility, direction, seg_pressure, seg_direction,
        perf_cell, well_index, parent, seg_head, well_mode, bhp_limit, guide_rate, group_of, group_target,
    ):
        n_well, n_seg = perf_cell.shape
        _, cx, cy = pressure.shape
        groups = group_target.shape[0]
        vmem = pl.BlockSpec(memory_space=pltpu.VMEM)
        dma = pltpu.SemaphoreType.DMA
        cells = jax.ShapeDtypeStruct(old_mass.shape, F32)
        segs = jax.ShapeDtypeStruct((n_well // ny, n_seg), F32)
        row = lambda x: x.reshape(1, -1)
        return pl.pallas_call(
            lambda *refs: kernel(nx, ny, n_well, *refs),
            out_shape=(cells, cells, segs, segs, jax.ShapeDtypeStruct((3, groups), F32)),
            in_specs=[vmem] * 17,
            out_specs=(vmem,) * 5,
            scratch_shapes=[
                pltpu.VMEM((12 * cx, 2 * cy), BF16),
                pltpu.VMEM((6, n_well, n_seg), F32),
                pltpu.VMEM((6, n_well, n_seg), F32),
                pltpu.VMEM((8, 2, cx + 8, cy), F32),
                pltpu.VMEM((6, 2, cx + 8, cy), F32),
                pltpu.VMEM((cx, cy), F32),
                pltpu.VMEM((4, 16, cy), F32),
                pltpu.VMEM((4, 16, cy), F32),
                pltpu.VMEM((ny, 8, n_seg), F32),
                pltpu.VMEM((ny, 8, n_seg), F32),
                pltpu.VMEM((8, groups), F32),
                pltpu.VMEM((nx, 8, groups), F32),
                dma((4,)), dma((4,)), dma((ny,)), dma((ny,)), dma((nx,)), dma((nx,)),
            ],
            compiler_params=pltpu.CompilerParams(
                collective_id=0, has_side_effects=True, vmem_limit_bytes=48 * 1024 * 1024
            ),
            name="newton",
        )(
            pressure, saturations, old_mass, pore_volume, transmissibility, direction, seg_pressure, seg_direction,
            perf_cell, well_index, parent, seg_head, row(well_mode), row(bhp_limit), row(guide_rate), row(group_of),
            row(group_target),
        )

    placed = (
        P(None, "gx", "gy"),
        P(None, None, "gx", "gy"),
        P(None, None, "gx", "gy"),
        P(None, "gx", "gy"),
        P(None, None, "gx", "gy"),
        P(None, None, "gx", "gy"),
        P("gx", None),
        P("gx", None),
        P("gx", None),
        P("gx", None),
        P("gx", None),
        P("gx", None),
        P("gx"),
        P("gx"),
        P("gx"),
        P("gx", None),
        P(),
    )
    return jax.shard_map(
        per_device,
        mesh=mesh,
        in_specs=placed,
        out_specs=(
            P(None, None, "gx", "gy"),
            P(None, None, "gx", "gy"),
            P(("gx", "gy"), None),
            P(("gx", "gy"), None),
            P(),
        ),
        check_vma=False,
    )
```

```python
import jax
import jax.numpy as jnp
from jax import lax
from jax.experimental import pallas as pl
from jax.experimental.pallas import tpu as pltpu
from jax.sharding import PartitionSpec as P

COMPRESS = (0.05, 0.2, 1.0)
VISCOSITY = (0.5, 1.0, 0.2)
DENSITY = (1.0, 0.8, 0.2)
ROCK_COMP = 0.01
GRAVITY = 0.05
UPWIND_WIDTH = 0.02
FRICTION = 0.002
RATE_SCALE = 0.1

MESH = pl.DeviceIdType.MESH
F32 = jnp.float32
BF16 = jnp.bfloat16
NT = (((1,), (1,)), ((), ()))

CH = 32
GATHER_UNROLL = 8
LOAD_ORDER = (0, 1, 5, 8, 9, 6, 7, 15, 14, 16, 4, 2, 3, 10, 11, 12, 13)


def iota(shape, dim):
    return lax.broadcasted_iota(jnp.int32, shape, dim)


def split2(x):
    high = x.astype(BF16).astype(F32)
    return high, x - high


def split3(x):
    high = x.astype(BF16).astype(F32)
    rest = x - high
    mid = rest.astype(BF16).astype(F32)
    return high, mid, rest - mid


def mobilities(press, water, gas, dpress, dwater, dgas):
    satur = (water, 1.0 - water - gas, gas)
    dsatur = (dwater, -dwater - dgas, dgas)
    volumes, mobil, dmobil = [], [], []
    for a in range(3):
        volume = jnp.exp(COMPRESS[a] * (press - 1.0))
        scaled = satur[a] * volume * (1.0 / VISCOSITY[a])
        volumes.append(volume)
        mobil.append(satur[a] * scaled)
        dmobil.append(scaled * (2.0 * dsatur[a] + COMPRESS[a] * satur[a] * dpress))
    return satur, dsatur, volumes, mobil, dmobil


def upwinding(potential, dpotential):
    half = jnp.tanh(potential * (0.5 / UPWIND_WIDTH))
    upwind = 0.5 + 0.5 * half
    dupwind = (1.0 - half * half) * (0.25 / UPWIND_WIDTH) * dpotential
    return upwind, dupwind


def face(trans, pot, dpot, up, dup, m_in, m_out, dm_in, dm_out):
    jump = m_in - m_out
    mean = m_out + up * jump
    dmean = dm_out + up * (dm_in - dm_out) + dup * jump
    flow = trans * pot
    return flow * mean, flow * dmean + (trans * dpot) * mean


def kernel(nx, ny, *refs):
    hbm, refs = refs[:17], refs[17:]
    (res, jvp, seg_res, seg_jvp, grates), refs = refs[:5], refs[5:]
    held, refs = refs[:17], refs[17:]
    (
        mhl, gath, mob, colf, edge, halo_tx, halo_rx, msg, rx1, msg2, rx2,
        s_in, s_h, r_h, s_1, r_1, s_2, r_2,
    ) = refs
    (
        press, sat, old, pore, trans, direc, seg_p, seg_d, perf, windex, parent, head,
        mode, bhp, guide, group, gtarget,
    ) = held
    loads = [pltpu.make_async_copy(hbm[i], held[i], s_in.at[i]) for i in range(17)]
    for i in LOAD_ORDER:
        loads[i].start()
    waited = set()

    def need(*which):
        for i in which:
            if i not in waited:
                waited.add(i)
                loads[i].wait()

    n_well = perf.shape[0]
    cx, cy = press.shape[1], press.shape[2]
    gx, gy = lax.axis_index("gx"), lax.axis_index("gy")
    share = n_well // ny

    barrier = pltpu.get_barrier_semaphore()
    for k in range(1, ny):
        pl.semaphore_signal(barrier, inc=1, device_id={"gy": lax.rem(gy + k, ny)}, device_id_type=MESH)
    for k in range(1, nx):
        pl.semaphore_signal(barrier, inc=1, device_id={"gx": lax.rem(gx + k, nx)}, device_id_type=MESH)

    need(0, 1, 5)
    for l in range(2):
        for q in range(6):
            block = (press.at[l], sat.at[0, l], sat.at[1, l], direc.at[0, l], direc.at[1, l], direc.at[2, l])[q]
            high, low = split2(block[...])
            at = (q * 2 + l) * cx
            mhl[at:at + cx, 0:cy] = high.astype(BF16)
            mhl[at:at + cx, cy:2 * cy] = low.astype(BF16)

    def send(src, dst, s_sem, r_sem, where):
        copy = pltpu.make_async_remote_copy(
            src_ref=src, dst_ref=dst, send_sem=s_sem, recv_sem=r_sem, device_id=where, device_id_type=MESH
        )
        copy.start()
        return copy

    need(8)
    all_rows = cy * ny
    shift = all_rows.bit_length() - 1
    first_row = gy * cy

    def split_cell(cell):
        return lax.shift_right_logical(cell, shift), (cell & (all_rows - 1)) - first_row

    def gather(c, _):
        w = 2 * c
        cell = jnp.concatenate([perf[pl.ds(w, 1), :], perf[pl.ds(w + 1, 1), :]], axis=1)
        col, row = split_cell(cell)
        hot = (iota((cy, cell.shape[1]), 0) == row).astype(F32).astype(BF16)
        hot = jnp.concatenate([hot, hot], axis=0)
        pick = iota((2 * cx, cell.shape[1]), 0) == col
        for q in range(6):
            got = jnp.dot(mhl[q * 2 * cx:(q + 1) * 2 * cx, :], hot, preferred_element_type=F32)
            got = jnp.sum(jnp.where(pick, got, 0.0), axis=0, keepdims=True)
            half = cell.shape[1] // 2
            gath[q, pl.ds(w, 1), :] = got[:, :half]
            gath[q, pl.ds(w + 1, 1), :] = got[:, half:]
        return 0

    lax.fori_loop(0, n_well // 2, gather, 0, unroll=GATHER_UNROLL)

    need(9, 6, 7, 15, 14, 16)
    col, row = split_cell(perf[...])
    weight = jnp.where((row >= 0) & (row < cy), windex[...], 0.0)
    values = [gath[q] for q in range(6)]
    _, _, _, m, dm = mobilities(*values)
    drop = weight * (values[0] - seg_p[...])
    ddrop = weight * (values[3] - seg_d[...])
    well = iota((n_well, n_well), 0) == iota((n_well, n_well), 1)
    group_col = jnp.sum(jnp.where(well, group[...].astype(F32), 0.0), axis=1, keepdims=True)
    guide_col = jnp.sum(jnp.where(well, guide[...], 0.0), axis=1, keepdims=True)
    groups = gtarget.shape[1]
    member = group_col == iota((n_well, groups), 1).astype(F32)
    guide_part = jnp.sum(jnp.where(member, guide_col, 0.0), axis=0, keepdims=True)
    total = jnp.zeros_like(drop)
    dtotal = jnp.zeros_like(drop)
    parts = []
    for a in range(3):
        rate = m[a] * drop
        drate = dm[a] * drop + m[a] * ddrop
        gath[a] = rate
        gath[3 + a] = drate
        total = total + rate
        dtotal = dtotal + drate
        by_well = jnp.sum(rate, axis=1, keepdims=True)
        parts.append(jnp.sum(jnp.where(member, by_well, 0.0), axis=0, keepdims=True))
    tail = jnp.concatenate(parts + [jnp.zeros_like(parts[0])], axis=0)
    for d in range(ny):
        msg[d, 0:2, :] = total[2 * d:2 * d + 2]
        msg[d, 2:4, :] = dtotal[2 * d:2 * d + 2]
        msg[d, 4:8, :] = tail
    pl.semaphore_wait(barrier, nx + ny - 2)
    first = []
    for k in range(1, ny):
        to = lax.rem(gy + k, ny)
        first.append(send(msg.at[to], rx1.at[k], s_1.at[k], r_1.at[k], {"gy": to}))

    need(4)
    lane = iota((cx, cy), 1)
    acc = jnp.zeros((cx, cy), F32)
    for l in range(2):
        for q in range(7):
            block = (
                press.at[l], sat.at[0, l], sat.at[1, l], direc.at[0, l], direc.at[1, l], direc.at[2, l], trans.at[0, l]
            )[q]
            row = 2 * q + l
            halo_tx[0, row:row + 1, :] = block[cx - 1:cx, :]
            halo_tx[1, row:row + 1, :] = block[0:1, :]
            lanes = trans[1, l] if q == 6 else block[...]
            acc = jnp.where(lane == row, lanes[:, cy - 1:cy], acc)
            acc = jnp.where(lane == 16 + row, lanes[:, 0:1], acc)
    flipped = acc.T
    halo_tx[2] = flipped[0:16]
    halo_tx[3] = flipped[16:32]
    halo_tx[0, 14:16, :] = jnp.zeros((2, cy), F32)
    halo_tx[1, 14:16, :] = jnp.zeros((2, cy), F32)
    targets = (
        {"gx": lax.rem(gx + 1, nx)},
        {"gx": lax.rem(gx + nx - 1, nx)},
        {"gy": lax.rem(gy + 1, ny)},
        {"gy": lax.rem(gy + ny - 1, ny)},
    )
    halo = [send(halo_tx.at[f], halo_rx.at[f], s_h.at[f], r_h.at[f], targets[f]) for f in range(4)]

    need(2, 3)
    last = (iota((CH, cy), 1) == cy - 1)
    for l in range(2):
        for q in range(8):
            mob[q, l, cx:cx + 8, :] = jnp.zeros((8, cy), F32)
    colf[:, :, 0:8, :] = jnp.zeros((6, 2, 8, cy), F32)
    for c in range(cx // CH):
        at = slice(c * CH, (c + 1) * CH)
        props = []
        for l in range(2):
            v = (press[l, at], sat[0, l, at], sat[1, l, at], direc[0, l, at], direc[1, l, at], direc[2, l, at])
            satur, dsatur, volume, m, dm = mobilities(*v)
            rock = (1.0 + ROCK_COMP * (v[0] - 1.0)) * pore[l, at]
            drock = ROCK_COMP * v[3] * pore[l, at]
            mob[6, l, at, :] = v[0]
            mob[7, l, at, :] = v[3]
            pot = v[0] - pltpu.roll(v[0], cy - 1, 1)
            dpot = v[3] - pltpu.roll(v[3], cy - 1, 1)
            t = jnp.where(last, 0.0, trans[1, l, at])
            up, dup = upwinding(pot, dpot)
            for a in range(3):
                mob[a, l, at, :] = m[a]
                mob[3 + a, l, at, :] = dm[a]
                mass = satur[a] * volume[a]
                dmass = (dsatur[a] + COMPRESS[a] * satur[a] * v[3]) * volume[a]
                f, df = face(
                    t, pot, dpot, up, dup, m[a], pltpu.roll(m[a], cy - 1, 1), dm[a], pltpu.roll(dm[a], cy - 1, 1)
                )
                res[a, l, at, :] = rock * mass - old[a, l, at] + (f - pltpu.roll(f, 1, 1))
                jvp[a, l, at, :] = drock * mass + rock * dmass + (df - pltpu.roll(df, 1, 1))
            props.append((v[0], v[3], m, dm))
        (p0, d0, m0, dm0), (p1, d1, m1, dm1) = props
        t = trans[2, 0, at]
        for a in range(3):
            pot = p0 - p1 + DENSITY[a] * GRAVITY
            dpot = d0 - d1
            up, dup = upwinding(pot, dpot)
            f, df = face(t, pot, dpot, up, dup, m0[a], m1[a], dm0[a], dm1[a])
            res[a, 0, at, :] += f
            jvp[a, 0, at, :] += df
            res[a, 1, at, :] -= f
            jvp[a, 1, at, :] -= df

    for l in range(2):
        for c in range(cx // CH):
            at = slice(c * CH, (c + 1) * CH)
            nxt = slice(c * CH + 1, (c + 1) * CH + 1)
            here = slice(c * CH + 8, (c + 1) * CH + 8)
            t = trans[0, l, at]
            if c == cx // CH - 1:
                t = jnp.where(iota((CH, cy), 0) == CH - 1, 0.0, t)
            pot = mob[6, l, at] - mob[6, l, nxt]
            dpot = mob[7, l, at] - mob[7, l, nxt]
            up, dup = upwinding(pot, dpot)
            for a in range(3):
                f, df = face(
                    t, pot, dpot, up, dup, mob[a, l, at], mob[a, l, nxt], mob[3 + a, l, at], mob[3 + a, l, nxt]
                )
                colf[a, l, here, :] = f
                colf[3 + a, l, here, :] = df
        for c in range(cx // CH):
            at = slice(c * CH, (c + 1) * CH)
            here = slice(c * CH + 8, (c + 1) * CH + 8)
            prev = slice(c * CH + 7, (c + 1) * CH + 7)
            for a in range(3):
                res[a, l, at, :] += colf[a, l, here] - colf[a, l, prev]
                jvp[a, l, at, :] += colf[3 + a, l, here] - colf[3 + a, l, prev]

    need(10)
    n_seg = perf.shape[1]
    links, reaches = [], []
    for i in range(share):
        above = parent[pl.ds(gy * share + i, 1), :]
        down = iota((n_seg, n_seg), 0)
        link = down == above
        reach = jnp.where(link | (down == iota((n_seg, n_seg), 1)), 1.0, 0.0).astype(BF16)
        for _ in range((n_seg - 1).bit_length()):
            square = jnp.dot(reach, reach, preferred_element_type=F32)
            reach = jnp.minimum(square, 1.0).astype(BF16)
        links.append(jnp.where(link, 1.0, 0.0).astype(BF16))
        reaches.append(reach)

    sums = msg[gy]
    for k in range(1, ny):
        first[k - 1].wait_recv()
        sums = sums + rx1[k]
    msg2[0:3, :] = sums[4:7]
    msg2[3:4, :] = guide_part
    msg2[4:8, :] = jnp.zeros((4, groups), F32)
    second = []
    for k in range(1, nx):
        second.append(send(msg2, rx2.at[k], s_2.at[k], r_2.at[k], {"gx": lax.rem(gx + k, nx)}))

    flows, aboves, owns = [], [], []
    pad = (jnp.zeros((2, n_seg), F32),)
    for i in range(share):
        w = gy * share + i
        vals = jnp.concatenate(split3(sums[i:i + 1]) + split3(sums[2 + i:3 + i]) + pad, axis=0).astype(BF16)
        flow = lax.dot_general(vals, reaches[i], NT, preferred_element_type=F32)
        own = (seg_p[pl.ds(w, 1), :], seg_d[pl.ds(w, 1), :])
        vals = jnp.concatenate(split3(own[0]) + split3(own[1]) + pad, axis=0).astype(BF16)
        above = jnp.dot(vals, links[i], preferred_element_type=F32)
        flows.append((flow[0:1] + flow[1:2] + flow[2:3], flow[3:4] + flow[4:5] + flow[5:6]))
        aboves.append((above[0:1] + above[1:2] + above[2:3], above[3:4] + above[4:5] + above[5:6]))
        owns.append(own)

    hots, sides = [], [[] for _ in range(6)]
    for w in range(n_well):
        col, row = split_cell(perf[w:w + 1, :])
        hot = (iota((2 * cx, n_seg), 0) == col).astype(F32).astype(BF16)
        hots += [hot, hot]
        hit = (iota((cy, n_seg), 0) == row).astype(F32).astype(BF16).reshape(cy // 16, 16, n_seg)
        for q in range(6):
            for part in split2(gath[q, w:w + 1, :]):
                wide = jnp.broadcast_to(part, (16, n_seg)).astype(BF16)
                sides[q].append((hit * wide[None]).reshape(cy, n_seg))
    hot = jnp.concatenate(hots, axis=1)
    for a in range(3):
        spread = jnp.concatenate(
            [jnp.concatenate(sides[a], axis=1), jnp.concatenate(sides[3 + a], axis=1)], axis=0
        )
        out = lax.dot_general(hot, spread, NT, preferred_element_type=F32)
        for l in range(2):
            res[a, l] += out[l * cx:(l + 1) * cx, :cy]
            jvp[a, l] += out[l * cx:(l + 1) * cx, cy:]

    for f in range(4):
        halo[f].wait_recv()
    ins, outs = [], []
    for q in range(7):
        r = slice(2 * q, 2 * q + 2)
        ins.append(jnp.concatenate([halo_rx[0, r], halo_tx[0, r], halo_rx[2, r], halo_tx[2, r]], axis=0))
        outs.append(jnp.concatenate([halo_tx[1, r], halo_rx[1, r], halo_tx[3, r], halo_rx[3, r]], axis=0))
    side = iota((8, cy), 0) // 2
    outer = (
        ((side == 0) & (gx == 0)) | ((side == 1) & (gx == nx - 1))
        | ((side == 2) & (gy == 0)) | ((side == 3) & (gy == ny - 1))
    )
    t = jnp.where(outer, 0.0, ins[6])
    pot, dpot = ins[0] - outs[0], ins[3] - outs[3]
    up, dup = upwinding(pot, dpot)
    m_in, m_out = mobilities(*ins[:6]), mobilities(*outs[:6])
    faces = [
        face(t, pot, dpot, up, dup, m_in[3][a], m_out[3][a], m_in[4][a], m_out[4][a]) for a in range(3)
    ]
    edge[...] = jnp.zeros((cx, cy), F32)
    for a in range(3):
        for o, out in enumerate((res, jvp)):
            for l in range(2):
                out[a, l, 0:1, :] -= faces[a][o][l:l + 1]
                out[a, l, cx - 1:cx, :] += faces[a][o][2 + l:3 + l]
            edge[(2 * a + o) * 4:(2 * a + o) * 4 + 4, :] = faces[a][o][4:8]
    turned = edge[...].T
    for a in range(3):
        for o, out in enumerate((res, jvp)):
            for l in range(2):
                at = (2 * a + o) * 4 + l
                delta = jnp.where(lane == 0, -turned[:, at:at + 1], 0.0)
                out[a, l] += jnp.where(lane == cy - 1, turned[:, at + 2:at + 3], delta)

    need(11, 12, 13)
    everything = msg2[...]
    for k in range(1, nx):
        second[k - 1].wait_recv()
        everything = everything + rx2[k]
    grates[...] = everything[0:3]
    guide_total = everything[3:4]

    wells = iota((1, n_well), 1)
    segs = iota((1, n_seg), 1)
    names = iota((1, groups), 1).astype(F32)
    for i in range(share):
        w = gy * share + i
        mine = wells == w
        pick = lambda ref: jnp.sum(jnp.where(mine, ref[...].astype(F32), 0.0), axis=1, keepdims=True)
        chosen = names == pick(group)
        named = lambda row: jnp.sum(jnp.where(chosen, row, 0.0), axis=1, keepdims=True)
        target = named(gtarget[...]) * pick(guide) / named(guide_total)
        rated = pick(mode) == 1.0
        (flow, dflow), (above, dabove), (own, down) = flows[i], aboves[i], owns[i]
        inner = own - above - head[pl.ds(w, 1), :] - FRICTION * flow
        root = jnp.where(rated, RATE_SCALE * (flow - target), own - pick(bhp))
        seg_res[i:i + 1, :] = jnp.where(segs == 0, root, inner)
        inner = down - dabove - FRICTION * dflow
        root = jnp.where(rated, RATE_SCALE * dflow, down)
        seg_jvp[i:i + 1, :] = jnp.where(segs == 0, root, inner)

    for copy in halo + first + second:
        copy.wait_send()


def write_out(*refs):
    copies = [pltpu.make_async_copy(refs[i], refs[5 + i], refs[10].at[i]) for i in range(5)]
    for copy in copies:
        copy.start()
    for copy in copies:
        copy.wait()


def solution(mesh):
    nx, ny = mesh.shape["gx"], mesh.shape["gy"]

    def per_device(
        pressure, saturations, old_mass, pore_volume, transmissibility, direction, seg_pressure, seg_direction,
        perf_cell, well_index, parent, seg_head, well_mode, bhp_limit, guide_rate, group_of, group_target,
    ):
        n_well, n_seg = perf_cell.shape
        _, cx, cy = pressure.shape
        groups = group_target.shape[0]
        vmem = pl.BlockSpec(memory_space=pltpu.VMEM)
        hbm = pl.BlockSpec(memory_space=pltpu.HBM)
        dma = pltpu.SemaphoreType.DMA
        cells = jax.ShapeDtypeStruct(old_mass.shape, F32)
        segs = jax.ShapeDtypeStruct((n_well // ny, n_seg), F32)
        outs = (cells, cells, segs, segs, jax.ShapeDtypeStruct((3, groups), F32))
        row = lambda x: x.reshape(1, -1)
        args = (
            pressure, saturations, old_mass, pore_volume, transmissibility, direction, seg_pressure, seg_direction,
            perf_cell, well_index, parent, seg_head, row(well_mode), row(bhp_limit), row(guide_rate), row(group_of),
            row(group_target),
        )
        made = pl.pallas_call(
            lambda *refs: kernel(nx, ny, *refs),
            out_shape=tuple(pltpu.VMEM(x.shape, x.dtype) for x in outs),
            in_specs=[hbm] * 17,
            out_specs=(vmem,) * 5,
            scratch_shapes=[pltpu.VMEM(x.shape, x.dtype) for x in args] + [
                pltpu.VMEM((12 * cx, 2 * cy), BF16),
                pltpu.VMEM((6, n_well, n_seg), F32),
                pltpu.VMEM((8, 2, cx + 8, cy), F32),
                pltpu.VMEM((6, 2, cx + 8, cy), F32),
                pltpu.VMEM((cx, cy), F32),
                pltpu.VMEM((4, 16, cy), F32),
                pltpu.VMEM((4, 16, cy), F32),
                pltpu.VMEM((ny, 8, n_seg), F32),
                pltpu.VMEM((ny, 8, n_seg), F32),
                pltpu.VMEM((8, groups), F32),
                pltpu.VMEM((nx, 8, groups), F32),
                dma((17,)), dma((4,)), dma((4,)), dma((ny,)), dma((ny,)), dma((nx,)), dma((nx,)),
            ],
            compiler_params=pltpu.CompilerParams(
                collective_id=0, has_side_effects=True, vmem_limit_bytes=60 * 1024 * 1024
            ),
            name="newton",
        )(*[pltpu.with_memory_space_constraint(x, pltpu.HBM) for x in args])
        return pl.pallas_call(
            write_out,
            out_shape=outs,
            in_specs=[vmem] * 5,
            out_specs=(hbm,) * 5,
            scratch_shapes=[dma((5,))],
            compiler_params=pltpu.CompilerParams(vmem_limit_bytes=1024 * 1024),
            name="write_out",
        )(*[pltpu.with_memory_space_constraint(x, pltpu.VMEM) for x in made])

    placed = (
        P(None, "gx", "gy"),
        P(None, None, "gx", "gy"),
        P(None, None, "gx", "gy"),
        P(None, "gx", "gy"),
        P(None, None, "gx", "gy"),
        P(None, None, "gx", "gy"),
        P("gx", None),
        P("gx", None),
        P("gx", None),
        P("gx", None),
        P("gx", None),
        P("gx", None),
        P("gx"),
        P("gx"),
        P("gx"),
        P("gx", None),
        P(),
    )
    return jax.shard_map(
        per_device,
        mesh=mesh,
        in_specs=placed,
        out_specs=(
            P(None, None, "gx", "gy"),
            P(None, None, "gx", "gy"),
            P(("gx", "gy"), None),
            P(("gx", "gy"), None),
            P(),
        ),
        check_vma=False,
    )
```

```python
import jax
import jax.numpy as jnp
from jax import lax
from jax.experimental import pallas as pl
from jax.experimental.pallas import tpu as pltpu
from jax.sharding import PartitionSpec as P

COMPRESS = (0.05, 0.2, 1.0)
VISCOSITY = (0.5, 1.0, 0.2)
DENSITY = (1.0, 0.8, 0.2)
ROCK_COMP = 0.01
GRAVITY = 0.05
UPWIND_WIDTH = 0.02
FRICTION = 0.002
RATE_SCALE = 0.1

MESH = pl.DeviceIdType.MESH
F32 = jnp.float32
BF16 = jnp.bfloat16
NT = (((1,), (1,)), ((), ()))

CH = 32
GATHER_BY_LANE = 10
GY_ORDER = (8, 7, 9, 6, 10, 5, 11, 4, 12, 3, 13, 2, 14, 1, 15)
GX_ORDER = (10, 6, 9, 11, 7, 5, 8, 14, 2, 13, 3, 12, 4, 1, 15)
LOAD_ORDER = (0, 1, 5, 8, 9, 6, 7, 15, 14, 16, 4, 2, 3, 10, 11, 12, 13)


def iota(shape, dim):
    return lax.broadcasted_iota(jnp.int32, shape, dim)


def split2(x):
    high = x.astype(BF16).astype(F32)
    return high, x - high


def split3(x):
    high = x.astype(BF16).astype(F32)
    rest = x - high
    mid = rest.astype(BF16).astype(F32)
    return high, mid, rest - mid


def mobilities(press, water, gas, dpress, dwater, dgas):
    satur = (water, 1.0 - water - gas, gas)
    dsatur = (dwater, -dwater - dgas, dgas)
    volumes, mobil, dmobil = [], [], []
    for a in range(3):
        volume = jnp.exp(COMPRESS[a] * (press - 1.0))
        scaled = satur[a] * volume * (1.0 / VISCOSITY[a])
        volumes.append(volume)
        mobil.append(satur[a] * scaled)
        dmobil.append(scaled * (2.0 * dsatur[a] + COMPRESS[a] * satur[a] * dpress))
    return satur, dsatur, volumes, mobil, dmobil


def upwinding(potential, dpotential):
    half = jnp.tanh(potential * (0.5 / UPWIND_WIDTH))
    upwind = 0.5 + 0.5 * half
    dupwind = (1.0 - half * half) * (0.25 / UPWIND_WIDTH) * dpotential
    return upwind, dupwind


def face(trans, pot, dpot, up, dup, m_in, m_out, dm_in, dm_out):
    jump = m_in - m_out
    mean = m_out + up * jump
    dmean = dm_out + up * (dm_in - dm_out) + dup * jump
    flow = trans * pot
    return flow * mean, flow * dmean + (trans * dpot) * mean


def partners(order, count):
    return [k for k in order if k < count] if count <= 16 else list(range(1, count))


def kernel(nx, ny, *refs):
    hbm, refs = refs[:17], refs[17:]
    (res, jvp, seg_res, seg_jvp, grates), refs = refs[:5], refs[5:]
    held, refs = refs[:17], refs[17:]
    (
        mhl, gath, mob, colf, edge, halo_tx, halo_rx, msg, rx1, msg2, rx2, part, rxp,
        s_in, s_h, r_h, s_1, r_1, s_2, r_2, s_p, r_p,
    ) = refs
    (
        press, sat, old, pore, trans, direc, seg_p, seg_d, perf, windex, parent, head,
        mode, bhp, guide, group, gtarget,
    ) = held
    loads = [pltpu.make_async_copy(hbm[i], held[i], s_in.at[i]) for i in range(17)]
    for i in LOAD_ORDER:
        loads[i].start()
    waited = set()

    def need(*which):
        for i in which:
            if i not in waited:
                waited.add(i)
                loads[i].wait()

    n_well = perf.shape[0]
    cx, cy = press.shape[1], press.shape[2]
    gx, gy = lax.axis_index("gx"), lax.axis_index("gy")
    share = n_well // ny

    barrier = pltpu.get_barrier_semaphore()
    for k in range(1, ny):
        pl.semaphore_signal(barrier, inc=1, device_id={"gy": lax.rem(gy + k, ny)}, device_id_type=MESH)
    for k in range(1, nx):
        pl.semaphore_signal(barrier, inc=1, device_id={"gx": lax.rem(gx + k, nx)}, device_id_type=MESH)

    cells = lambda q, l: (
        press.at[l], sat.at[0, l], sat.at[1, l], direc.at[0, l], direc.at[1, l], direc.at[2, l]
    )[q]
    for q in range(6):
        need((0, 1, 1, 5, 5, 5)[q])
        for l in range(2):
            high, low = split2(cells(q, l)[...])
            at = (q * 2 + l) * cx
            mhl[at:at + cx, 0:cy] = high.astype(BF16)
            mhl[at:at + cx, cy:2 * cy] = low.astype(BF16)

    def wait_all(landed, sem):
        pltpu.make_async_copy(landed, landed, sem.at[0]).wait()

    def send(src, dst, s_sem, r_sem, where):
        copy = pltpu.make_async_remote_copy(
            src_ref=src, dst_ref=dst, send_sem=s_sem, recv_sem=r_sem, device_id=where, device_id_type=MESH
        )
        copy.start()

    need(8)
    all_rows = cy * ny
    shift = all_rows.bit_length() - 1
    first_row = gy * cy

    def split_cell(cell):
        return lax.shift_right_logical(cell, shift), (cell & (all_rows - 1)) - first_row

    def by_product(w):
        cell = jnp.concatenate([perf[w:w + 1, :], perf[w + 1:w + 2, :]], axis=1)
        col, row = split_cell(cell)
        n = cell.shape[1]
        hot = (iota((cy, n), 0) == row).astype(F32).astype(BF16)
        hot = jnp.concatenate([hot, hot], axis=0)
        lines = [
            jnp.dot(mhl[q * 2 * cx:(q + 1) * 2 * cx, :], hot, preferred_element_type=F32) for q in range(6)
        ]
        found = [jnp.zeros((8, n), F32)] * 6
        offset = iota((8, n), 0) - col
        for i in range(2 * cx // 8):
            hit = offset == -8 * i
            found = [jnp.where(hit, lines[q][8 * i:8 * i + 8], found[q]) for q in range(6)]
        for q in range(6):
            line = jnp.sum(found[q], axis=0, keepdims=True)
            gath[q, w:w + 1, :] = line[:, :n // 2]
            gath[q, w + 1:w + 2, :] = line[:, n // 2:]

    def by_lane(w):
        col, row = split_cell(perf[w:w + 1, :])
        n = col.shape[1]
        lanes = jnp.broadcast_to(jnp.clip(row, 0, cy - 1), (8, n))
        offset = jnp.where((row >= 0) & (row < cy), iota((8, n), 0) - col, 1)
        found = [jnp.zeros((8, n), F32)] * 6
        for i in range(2 * cx // 8):
            l, r = divmod(8 * i, cx)
            hit = offset == -8 * i
            for q in range(6):
                line = jnp.take_along_axis(cells(q, l)[r:r + 8, :], lanes, axis=1, mode="promise_in_bounds")
                found[q] = jnp.where(hit, line, found[q])
        for q in range(6):
            gath[q, w:w + 1, :] = jnp.sum(found[q], axis=0, keepdims=True)

    for w in range(0, n_well - GATHER_BY_LANE, 2):
        by_product(w)
    for w in range(n_well - GATHER_BY_LANE, n_well):
        by_lane(w)

    need(9, 6, 7, 15, 14, 16)
    col, row = split_cell(perf[...])
    weight = jnp.where((row >= 0) & (row < cy), windex[...], 0.0)
    values = [gath[q] for q in range(6)]
    _, _, _, m, dm = mobilities(*values)
    drop = weight * (values[0] - seg_p[...])
    ddrop = weight * (values[3] - seg_d[...])
    well = iota((n_well, n_well), 0) == iota((n_well, n_well), 1)
    group_col = jnp.sum(jnp.where(well, group[...].astype(F32), 0.0), axis=1, keepdims=True)
    guide_col = jnp.sum(jnp.where(well, guide[...], 0.0), axis=1, keepdims=True)
    groups = gtarget.shape[1]
    member = group_col == iota((n_well, groups), 1).astype(F32)
    guide_part = jnp.sum(jnp.where(member, guide_col, 0.0), axis=0, keepdims=True)
    total = jnp.zeros_like(drop)
    dtotal = jnp.zeros_like(drop)
    parts = []
    for a in range(3):
        rate = m[a] * drop
        drate = dm[a] * drop + m[a] * ddrop
        gath[a] = rate
        gath[3 + a] = drate
        total = total + rate
        dtotal = dtotal + drate
        by_well = jnp.sum(rate, axis=1, keepdims=True)
        parts.append(jnp.sum(jnp.where(member, by_well, 0.0), axis=0, keepdims=True))
    for a in range(3):
        part[a:a + 1, :] = parts[a]
    pl.semaphore_wait(barrier, nx + ny - 2)
    for k in partners(GY_ORDER, ny):
        to = lax.rem(gy + k, ny)
        send(part.at[pl.ds(0, 3)], rxp.at[k, pl.ds(0, 3)], s_p.at[0], r_p.at[0], {"gy": to})
    for d in range(ny):
        msg[d, 0:2, :] = total[2 * d:2 * d + 2]
        msg[d, 2:4, :] = dtotal[2 * d:2 * d + 2]
    for k in partners(GY_ORDER, ny):
        to = lax.rem(gy + k, ny)
        send(msg.at[to, pl.ds(0, 4)], rx1.at[k, pl.ds(0, 4)], s_1.at[0], r_1.at[0], {"gy": to})
    need(4)
    lane = iota((cx, cy), 1)
    acc = jnp.zeros((cx, cy), F32)
    for l in range(2):
        for q in range(7):
            block = (
                press.at[l], sat.at[0, l], sat.at[1, l], direc.at[0, l], direc.at[1, l], direc.at[2, l], trans.at[0, l]
            )[q]
            row = 2 * q + l
            halo_tx[0, row:row + 1, :] = block[cx - 1:cx, :]
            halo_tx[1, row:row + 1, :] = block[0:1, :]
            lanes = trans[1, l] if q == 6 else block[...]
            acc = jnp.where(lane == row, lanes[:, cy - 1:cy], acc)
            acc = jnp.where(lane == 16 + row, lanes[:, 0:1], acc)
    flipped = acc.T
    halo_tx[2] = flipped[0:16]
    halo_tx[3] = flipped[16:32]
    halo_tx[0, 14:16, :] = jnp.zeros((2, cy), F32)
    halo_tx[1, 14:16, :] = jnp.zeros((2, cy), F32)
    targets = (
        {"gx": lax.rem(gx + 1, nx)},
        {"gx": lax.rem(gx + nx - 1, nx)},
        {"gy": lax.rem(gy + 1, ny)},
        {"gy": lax.rem(gy + ny - 1, ny)},
    )
    for f in range(4):
        send(halo_tx.at[f], halo_rx.at[f], s_h.at[0], r_h.at[0], targets[f])

    need(2, 3)
    last = (iota((CH, cy), 1) == cy - 1)
    for l in range(2):
        for q in range(8):
            mob[q, l, cx:cx + 8, :] = jnp.zeros((8, cy), F32)
    colf[:, :, 0:8, :] = jnp.zeros((6, 2, 8, cy), F32)
    for c in range(cx // CH):
        at = slice(c * CH, (c + 1) * CH)
        props = []
        for l in range(2):
            v = (press[l, at], sat[0, l, at], sat[1, l, at], direc[0, l, at], direc[1, l, at], direc[2, l, at])
            satur, dsatur, volume, m, dm = mobilities(*v)
            rock = (1.0 + ROCK_COMP * (v[0] - 1.0)) * pore[l, at]
            drock = ROCK_COMP * v[3] * pore[l, at]
            mob[6, l, at, :] = v[0]
            mob[7, l, at, :] = v[3]
            pot = v[0] - pltpu.roll(v[0], cy - 1, 1)
            dpot = v[3] - pltpu.roll(v[3], cy - 1, 1)
            t = jnp.where(last, 0.0, trans[1, l, at])
            up, dup = upwinding(pot, dpot)
            for a in range(3):
                mob[a, l, at, :] = m[a]
                mob[3 + a, l, at, :] = dm[a]
                mass = satur[a] * volume[a]
                dmass = (dsatur[a] + COMPRESS[a] * satur[a] * v[3]) * volume[a]
                f, df = face(
                    t, pot, dpot, up, dup, m[a], pltpu.roll(m[a], cy - 1, 1), dm[a], pltpu.roll(dm[a], cy - 1, 1)
                )
                res[a, l, at, :] = rock * mass - old[a, l, at] + (f - pltpu.roll(f, 1, 1))
                jvp[a, l, at, :] = drock * mass + rock * dmass + (df - pltpu.roll(df, 1, 1))
            props.append((v[0], v[3], m, dm))
        (p0, d0, m0, dm0), (p1, d1, m1, dm1) = props
        t = trans[2, 0, at]
        for a in range(3):
            pot = p0 - p1 + DENSITY[a] * GRAVITY
            dpot = d0 - d1
            up, dup = upwinding(pot, dpot)
            f, df = face(t, pot, dpot, up, dup, m0[a], m1[a], dm0[a], dm1[a])
            res[a, 0, at, :] += f
            jvp[a, 0, at, :] += df
            res[a, 1, at, :] -= f
            jvp[a, 1, at, :] -= df

    for l in range(2):
        for c in range(cx // CH):
            at = slice(c * CH, (c + 1) * CH)
            nxt = slice(c * CH + 1, (c + 1) * CH + 1)
            here = slice(c * CH + 8, (c + 1) * CH + 8)
            t = trans[0, l, at]
            if c == cx // CH - 1:
                t = jnp.where(iota((CH, cy), 0) == CH - 1, 0.0, t)
            pot = mob[6, l, at] - mob[6, l, nxt]
            dpot = mob[7, l, at] - mob[7, l, nxt]
            up, dup = upwinding(pot, dpot)
            for a in range(3):
                f, df = face(
                    t, pot, dpot, up, dup, mob[a, l, at], mob[a, l, nxt], mob[3 + a, l, at], mob[3 + a, l, nxt]
                )
                colf[a, l, here, :] = f
                colf[3 + a, l, here, :] = df
        for c in range(cx // CH):
            at = slice(c * CH, (c + 1) * CH)
            here = slice(c * CH + 8, (c + 1) * CH + 8)
            prev = slice(c * CH + 7, (c + 1) * CH + 7)
            for a in range(3):
                res[a, l, at, :] += colf[a, l, here] - colf[a, l, prev]
                jvp[a, l, at, :] += colf[3 + a, l, here] - colf[3 + a, l, prev]

    need(10)
    n_seg = perf.shape[1]
    links, reaches = [], []
    for i in range(share):
        above = parent[pl.ds(gy * share + i, 1), :]
        down = iota((n_seg, n_seg), 0)
        link = down == above
        reach = jnp.where(link | (down == iota((n_seg, n_seg), 1)), 1.0, 0.0).astype(BF16)
        for _ in range((n_seg - 1).bit_length()):
            square = jnp.dot(reach, reach, preferred_element_type=F32)
            reach = jnp.minimum(square, 1.0).astype(BF16)
        links.append(jnp.where(link, 1.0, 0.0).astype(BF16))
        reaches.append(reach)

    sums = part[0:3, :]
    wait_all(rxp.at[pl.ds(1, ny - 1), pl.ds(0, 3)], r_p)
    for k in range(1, ny):
        sums = sums + rxp[k, 0:3, :]
    msg2[0:3, :] = sums
    msg2[3:4, :] = guide_part
    for k in partners(GX_ORDER, nx):
        to = lax.rem(gx + k, nx)
        send(msg2.at[pl.ds(0, 4)], rx2.at[k, pl.ds(0, 4)], s_2.at[0], r_2.at[0], {"gx": to})

    hots, sides = [], [[] for _ in range(6)]
    for w in range(n_well):
        col, row = split_cell(perf[w:w + 1, :])
        hot = (iota((2 * cx, n_seg), 0) == col).astype(F32).astype(BF16)
        hots += [hot, hot]
        hit = (iota((cy, n_seg), 0) == row).astype(F32).astype(BF16).reshape(cy // 16, 16, n_seg)
        for q in range(6):
            for part in split2(gath[q, w:w + 1, :]):
                wide = jnp.broadcast_to(part, (16, n_seg)).astype(BF16)
                sides[q].append((hit * wide[None]).reshape(cy, n_seg))
    hot = jnp.concatenate(hots, axis=1)
    for a in range(3):
        spread = jnp.concatenate(
            [jnp.concatenate(sides[a], axis=1), jnp.concatenate(sides[3 + a], axis=1)], axis=0
        )
        out = lax.dot_general(hot, spread, NT, preferred_element_type=F32)
        for l in range(2):
            res[a, l] += out[l * cx:(l + 1) * cx, :cy]
            jvp[a, l] += out[l * cx:(l + 1) * cx, cy:]

    wait_all(halo_rx, r_h)
    ins, outs = [], []
    for q in range(7):
        r = slice(2 * q, 2 * q + 2)
        ins.append(jnp.concatenate([halo_rx[0, r], halo_tx[0, r], halo_rx[2, r], halo_tx[2, r]], axis=0))
        outs.append(jnp.concatenate([halo_tx[1, r], halo_rx[1, r], halo_tx[3, r], halo_rx[3, r]], axis=0))
    side = iota((8, cy), 0) // 2
    outer = (
        ((side == 0) & (gx == 0)) | ((side == 1) & (gx == nx - 1))
        | ((side == 2) & (gy == 0)) | ((side == 3) & (gy == ny - 1))
    )
    t = jnp.where(outer, 0.0, ins[6])
    pot, dpot = ins[0] - outs[0], ins[3] - outs[3]
    up, dup = upwinding(pot, dpot)
    m_in, m_out = mobilities(*ins[:6]), mobilities(*outs[:6])
    faces = [
        face(t, pot, dpot, up, dup, m_in[3][a], m_out[3][a], m_in[4][a], m_out[4][a]) for a in range(3)
    ]
    edge[...] = jnp.zeros((cx, cy), F32)
    for a in range(3):
        for o, out in enumerate((res, jvp)):
            for l in range(2):
                out[a, l, 0:1, :] -= faces[a][o][l:l + 1]
                out[a, l, cx - 1:cx, :] += faces[a][o][2 + l:3 + l]
            edge[(2 * a + o) * 4:(2 * a + o) * 4 + 4, :] = faces[a][o][4:8]
    turned = edge[...].T
    for a in range(3):
        for o, out in enumerate((res, jvp)):
            for l in range(2):
                at = (2 * a + o) * 4 + l
                delta = jnp.where(lane == 0, -turned[:, at:at + 1], 0.0)
                out[a, l] += jnp.where(lane == cy - 1, turned[:, at + 2:at + 3], delta)

    sums = msg[gy, 0:4, :]
    wait_all(rx1.at[pl.ds(1, ny - 1), pl.ds(0, 4)], r_1)
    for k in range(1, ny):
        sums = sums + rx1[k, 0:4, :]

    flows, aboves, owns = [], [], []
    pad = (jnp.zeros((2, n_seg), F32),)
    for i in range(share):
        w = gy * share + i
        vals = jnp.concatenate(split3(sums[i:i + 1]) + split3(sums[2 + i:3 + i]) + pad, axis=0).astype(BF16)
        flow = lax.dot_general(vals, reaches[i], NT, preferred_element_type=F32)
        own = (seg_p[pl.ds(w, 1), :], seg_d[pl.ds(w, 1), :])
        vals = jnp.concatenate(split3(own[0]) + split3(own[1]) + pad, axis=0).astype(BF16)
        above = jnp.dot(vals, links[i], preferred_element_type=F32)
        flows.append((flow[0:1] + flow[1:2] + flow[2:3], flow[3:4] + flow[4:5] + flow[5:6]))
        aboves.append((above[0:1] + above[1:2] + above[2:3], above[3:4] + above[4:5] + above[5:6]))
        owns.append(own)

    need(11, 12, 13)
    everything = msg2[0:4, :]
    wait_all(rx2.at[pl.ds(1, nx - 1), pl.ds(0, 4)], r_2)
    for k in range(1, nx):
        everything = everything + rx2[k, 0:4, :]
    grates[...] = everything[0:3]
    guide_total = everything[3:4]

    wells = iota((1, n_well), 1)
    segs = iota((1, n_seg), 1)
    names = iota((1, groups), 1).astype(F32)
    for i in range(share):
        w = gy * share + i
        mine = wells == w
        pick = lambda ref: jnp.sum(jnp.where(mine, ref[...].astype(F32), 0.0), axis=1, keepdims=True)
        chosen = names == pick(group)
        named = lambda row: jnp.sum(jnp.where(chosen, row, 0.0), axis=1, keepdims=True)
        target = named(gtarget[...]) * pick(guide) / named(guide_total)
        rated = pick(mode) == 1.0
        (flow, dflow), (above, dabove), (own, down) = flows[i], aboves[i], owns[i]
        inner = own - above - head[pl.ds(w, 1), :] - FRICTION * flow
        root = jnp.where(rated, RATE_SCALE * (flow - target), own - pick(bhp))
        seg_res[i:i + 1, :] = jnp.where(segs == 0, root, inner)
        inner = down - dabove - FRICTION * dflow
        root = jnp.where(rated, RATE_SCALE * dflow, down)
        seg_jvp[i:i + 1, :] = jnp.where(segs == 0, root, inner)

    wait_all(halo_rx, s_h)
    wait_all(rxp.at[pl.ds(1, ny - 1), pl.ds(0, 3)], s_p)
    wait_all(rx1.at[pl.ds(1, ny - 1), pl.ds(0, 4)], s_1)
    wait_all(rx2.at[pl.ds(1, nx - 1), pl.ds(0, 4)], s_2)


def write_out(*refs):
    copies = [pltpu.make_async_copy(refs[i], refs[5 + i], refs[10].at[i]) for i in range(5)]
    for copy in copies:
        copy.start()
    for copy in copies:
        copy.wait()


def solution(mesh):
    nx, ny = mesh.shape["gx"], mesh.shape["gy"]

    def per_device(
        pressure, saturations, old_mass, pore_volume, transmissibility, direction, seg_pressure, seg_direction,
        perf_cell, well_index, parent, seg_head, well_mode, bhp_limit, guide_rate, group_of, group_target,
    ):
        n_well, n_seg = perf_cell.shape
        _, cx, cy = pressure.shape
        groups = group_target.shape[0]
        vmem = pl.BlockSpec(memory_space=pltpu.VMEM)
        hbm = pl.BlockSpec(memory_space=pltpu.HBM)
        dma = pltpu.SemaphoreType.DMA
        cells = jax.ShapeDtypeStruct(old_mass.shape, F32)
        segs = jax.ShapeDtypeStruct((n_well // ny, n_seg), F32)
        outs = (cells, cells, segs, segs, jax.ShapeDtypeStruct((3, groups), F32))
        row = lambda x: x.reshape(1, -1)
        args = (
            pressure, saturations, old_mass, pore_volume, transmissibility, direction, seg_pressure, seg_direction,
            perf_cell, well_index, parent, seg_head, row(well_mode), row(bhp_limit), row(guide_rate), row(group_of),
            row(group_target),
        )
        made = pl.pallas_call(
            lambda *refs: kernel(nx, ny, *refs),
            out_shape=tuple(pltpu.VMEM(x.shape, x.dtype) for x in outs),
            in_specs=[hbm] * 17,
            out_specs=(vmem,) * 5,
            scratch_shapes=[pltpu.VMEM(x.shape, x.dtype) for x in args] + [
                pltpu.VMEM((12 * cx, 2 * cy), BF16),
                pltpu.VMEM((6, n_well, n_seg), F32),
                pltpu.VMEM((8, 2, cx + 8, cy), F32),
                pltpu.VMEM((6, 2, cx + 8, cy), F32),
                pltpu.VMEM((cx, cy), F32),
                pltpu.VMEM((4, 16, cy), F32),
                pltpu.VMEM((4, 16, cy), F32),
                pltpu.VMEM((ny, 8, n_seg), F32),
                pltpu.VMEM((ny, 8, n_seg), F32),
                pltpu.VMEM((8, groups), F32),
                pltpu.VMEM((nx, 8, groups), F32),
                pltpu.VMEM((8, groups), F32),
                pltpu.VMEM((ny, 8, groups), F32),
                dma((17,)), dma((1,)), dma((1,)), dma((1,)), dma((1,)), dma((1,)), dma((1,)), dma((1,)), dma((1,)),
            ],
            compiler_params=pltpu.CompilerParams(
                collective_id=0, has_side_effects=True, vmem_limit_bytes=60 * 1024 * 1024
            ),
            name="newton",
        )(*[pltpu.with_memory_space_constraint(x, pltpu.HBM) for x in args])
        return pl.pallas_call(
            write_out,
            out_shape=outs,
            in_specs=[vmem] * 5,
            out_specs=(hbm,) * 5,
            scratch_shapes=[dma((5,))],
            compiler_params=pltpu.CompilerParams(vmem_limit_bytes=1024 * 1024),
            name="write_out",
        )(*[pltpu.with_memory_space_constraint(x, pltpu.VMEM) for x in made])

    placed = (
        P(None, "gx", "gy"),
        P(None, None, "gx", "gy"),
        P(None, None, "gx", "gy"),
        P(None, "gx", "gy"),
        P(None, None, "gx", "gy"),
        P(None, None, "gx", "gy"),
        P("gx", None),
        P("gx", None),
        P("gx", None),
        P("gx", None),
        P("gx", None),
        P("gx", None),
        P("gx"),
        P("gx"),
        P("gx"),
        P("gx", None),
        P(),
    )
    return jax.shard_map(
        per_device,
        mesh=mesh,
        in_specs=placed,
        out_specs=(
            P(None, None, "gx", "gy"),
            P(None, None, "gx", "gy"),
            P(("gx", "gy"), None),
            P(("gx", "gy"), None),
            P(),
        ),
        check_vma=False,
    )
```

```python
import jax
import jax.numpy as jnp
from jax import lax
from jax.experimental import pallas as pl
from jax.experimental.pallas import tpu as pltpu
from jax.sharding import PartitionSpec as P

COMPRESS = (0.05, 0.2, 1.0)
VISCOSITY = (0.5, 1.0, 0.2)
DENSITY = (1.0, 0.8, 0.2)
ROCK_COMP = 0.01
GRAVITY = 0.05
UPWIND_WIDTH = 0.02
FRICTION = 0.002
RATE_SCALE = 0.1

MESH = pl.DeviceIdType.MESH
F32 = jnp.float32
BF16 = jnp.bfloat16
NT = (((1,), (1,)), ((), ()))

CH = 32
EXCHANGE_AT = 0.45
SPREAD_WELLS = 8
GATHER_BY_LANE = 10
GY_ORDER = (8, 7, 9, 6, 10, 5, 11, 4, 12, 3, 13, 2, 14, 1, 15)
GX_ORDER = (10, 6, 9, 11, 7, 5, 8, 14, 2, 13, 3, 12, 4, 1, 15)
LOAD_ORDER = (8, 0, 1, 9, 6, 15, 5, 7, 14, 16, 4, 2, 3, 10, 11, 12, 13)


def iota(shape, dim):
    return lax.broadcasted_iota(jnp.int32, shape, dim)


def split2(x):
    high = x.astype(BF16).astype(F32)
    return high, x - high


def split3(x):
    high = x.astype(BF16).astype(F32)
    rest = x - high
    mid = rest.astype(BF16).astype(F32)
    return high, mid, rest - mid


def mobilities(press, water, gas, dpress, dwater, dgas):
    satur = (water, 1.0 - water - gas, gas)
    dsatur = (dwater, -dwater - dgas, dgas)
    volumes, mobil, dmobil = [], [], []
    for a in range(3):
        volume = jnp.exp(COMPRESS[a] * (press - 1.0))
        scaled = satur[a] * volume * (1.0 / VISCOSITY[a])
        volumes.append(volume)
        mobil.append(satur[a] * scaled)
        dmobil.append(scaled * (2.0 * dsatur[a] + COMPRESS[a] * satur[a] * dpress))
    return satur, dsatur, volumes, mobil, dmobil


def upwinding(potential, dpotential):
    half = jnp.tanh(potential * (0.5 / UPWIND_WIDTH))
    upwind = 0.5 + 0.5 * half
    dupwind = (1.0 - half * half) * (0.25 / UPWIND_WIDTH) * dpotential
    return upwind, dupwind


def face(trans, pot, dpot, up, dup, m_in, m_out, dm_in, dm_out):
    jump = m_in - m_out
    mean = m_out + up * jump
    dmean = dm_out + up * (dm_in - dm_out) + dup * jump
    flow = trans * pot
    return flow * mean, flow * dmean + (trans * dpot) * mean


def weave(exchange, *strands):
    counts = [n for n, _ in strands]
    places = sorted((((i + 0.5) / n, j) for j, n in enumerate(counts) for i in range(n)))
    for i, (_, j) in enumerate(places):
        if i == round(EXCHANGE_AT * len(places)):
            exchange()
        next(strands[j][1])
    if EXCHANGE_AT == 1:
        exchange()


def spread_rates(perf, gath, split_cell, scat, cx, cy):
    n_well, n_seg = perf.shape

    def pieces():
        for start in range(0, n_well, SPREAD_WELLS):
            hots, hits = [], []
            for w in range(start, start + SPREAD_WELLS):
                col, row = split_cell(perf[w:w + 1, :])
                hot = (iota((2 * cx, n_seg), 0) == col).astype(F32).astype(BF16)
                hots += [hot, hot]
                hit = (iota((cy, n_seg), 0) == row).astype(F32).astype(BF16)
                hits.append(hit.reshape(cy // 16, 16, n_seg))
            hot = jnp.concatenate(hots, axis=1)
            for a in range(3):
                sides = []
                for q in (a, 3 + a):
                    side = []
                    for i in range(SPREAD_WELLS):
                        for part in split2(gath[q, start + i:start + i + 1, :]):
                            wide = jnp.broadcast_to(part, (16, n_seg)).astype(BF16)
                            side.append((hits[i] * wide[None]).reshape(cy, n_seg))
                    sides.append(jnp.concatenate(side, axis=1))
                out = lax.dot_general(hot, jnp.concatenate(sides, axis=0), NT, preferred_element_type=F32)
                if start == 0:
                    scat[a] = out
                else:
                    scat[a] += out
                yield

    return 3 * (n_well // SPREAD_WELLS), pieces()


def descent(parent, first, share, links, reaches):
    n_seg = parent.shape[1]
    levels = (n_seg - 1).bit_length()

    def pieces():
        down = iota((n_seg, n_seg), 0)
        for i in range(share):
            link = down == parent[pl.ds(first + i, 1), :]
            links.append(jnp.where(link, 1.0, 0.0).astype(BF16))
            reach = jnp.where(link | (down == iota((n_seg, n_seg), 1)), 1.0, 0.0).astype(BF16)
            reaches.append(reach)
        for _ in range(levels):
            squares = [jnp.dot(reach, reach, preferred_element_type=F32) for reach in reaches]
            reaches[:] = [jnp.minimum(square, 1.0).astype(BF16) for square in squares]
            yield

    return levels, pieces()


def cell_terms(press, sat, old, pore, trans, direc, res, jvp, mob, colf):
    cx, cy = press.shape[1], press.shape[2]
    steps = cx // CH

    def pieces():
        last = (iota((CH, cy), 1) == cy - 1)
        for l in range(2):
            for q in range(8):
                mob[q, l, cx:cx + 8, :] = jnp.zeros((8, cy), F32)
        colf[:, :, 0:8, :] = jnp.zeros((6, 2, 8, cy), F32)
        for c in range(cx // CH):
            at = slice(c * CH, (c + 1) * CH)
            props = []
            for l in range(2):
                v = (press[l, at], sat[0, l, at], sat[1, l, at], direc[0, l, at], direc[1, l, at], direc[2, l, at])
                satur, dsatur, volume, m, dm = mobilities(*v)
                rock = (1.0 + ROCK_COMP * (v[0] - 1.0)) * pore[l, at]
                drock = ROCK_COMP * v[3] * pore[l, at]
                mob[6, l, at, :] = v[0]
                mob[7, l, at, :] = v[3]
                pot = v[0] - pltpu.roll(v[0], cy - 1, 1)
                dpot = v[3] - pltpu.roll(v[3], cy - 1, 1)
                t = jnp.where(last, 0.0, trans[1, l, at])
                up, dup = upwinding(pot, dpot)
                for a in range(3):
                    mob[a, l, at, :] = m[a]
                    mob[3 + a, l, at, :] = dm[a]
                    mass = satur[a] * volume[a]
                    dmass = (dsatur[a] + COMPRESS[a] * satur[a] * v[3]) * volume[a]
                    f, df = face(
                        t, pot, dpot, up, dup, m[a], pltpu.roll(m[a], cy - 1, 1), dm[a], pltpu.roll(dm[a], cy - 1, 1)
                    )
                    res[a, l, at, :] = rock * mass - old[a, l, at] + (f - pltpu.roll(f, 1, 1))
                    jvp[a, l, at, :] = drock * mass + rock * dmass + (df - pltpu.roll(df, 1, 1))
                props.append((v[0], v[3], m, dm))
            (p0, d0, m0, dm0), (p1, d1, m1, dm1) = props
            t = trans[2, 0, at]
            for a in range(3):
                pot = p0 - p1 + DENSITY[a] * GRAVITY
                dpot = d0 - d1
                up, dup = upwinding(pot, dpot)
                f, df = face(t, pot, dpot, up, dup, m0[a], m1[a], dm0[a], dm1[a])
                res[a, 0, at, :] += f
                jvp[a, 0, at, :] += df
                res[a, 1, at, :] -= f
                jvp[a, 1, at, :] -= df
            yield

        for l in range(2):
            for c in range(cx // CH):
                at = slice(c * CH, (c + 1) * CH)
                nxt = slice(c * CH + 1, (c + 1) * CH + 1)
                here = slice(c * CH + 8, (c + 1) * CH + 8)
                t = trans[0, l, at]
                if c == cx // CH - 1:
                    t = jnp.where(iota((CH, cy), 0) == CH - 1, 0.0, t)
                pot = mob[6, l, at] - mob[6, l, nxt]
                dpot = mob[7, l, at] - mob[7, l, nxt]
                up, dup = upwinding(pot, dpot)
                for a in range(3):
                    f, df = face(
                        t, pot, dpot, up, dup, mob[a, l, at], mob[a, l, nxt], mob[3 + a, l, at], mob[3 + a, l, nxt]
                    )
                    colf[a, l, here, :] = f
                    colf[3 + a, l, here, :] = df
                yield
            for c in range(cx // CH):
                at = slice(c * CH, (c + 1) * CH)
                here = slice(c * CH + 8, (c + 1) * CH + 8)
                prev = slice(c * CH + 7, (c + 1) * CH + 7)
                for a in range(3):
                    res[a, l, at, :] += colf[a, l, here] - colf[a, l, prev]
                    jvp[a, l, at, :] += colf[3 + a, l, here] - colf[3 + a, l, prev]
                yield

    return 5 * steps, pieces()


def partners(order, count):
    return [k for k in order if k < count] if count <= 16 else list(range(1, count))


def kernel(nx, ny, *refs):
    hbm, refs = refs[:17], refs[17:]
    (res, jvp, seg_res, seg_jvp, grates), refs = refs[:5], refs[5:]
    held, refs = refs[:17], refs[17:]
    (
        mhl, gath, mob, colf, edge, halo_tx, halo_rx, msg, rx1, msg2, rx2, part, rxp, scat, aims, rxg,
        s_in, s_h, r_h, s_1, r_1, s_2, r_2, s_p, r_p, s_g, r_g,
    ) = refs
    (
        press, sat, old, pore, trans, direc, seg_p, seg_d, perf, windex, parent, head,
        mode, bhp, guide, group, gtarget,
    ) = held
    loads = [pltpu.make_async_copy(hbm[i], held[i], s_in.at[i]) for i in range(17)]
    for i in LOAD_ORDER:
        loads[i].start()
    waited = set()

    def need(*which):
        for i in which:
            if i not in waited:
                waited.add(i)
                loads[i].wait()

    n_well = perf.shape[0]
    cx, cy = press.shape[1], press.shape[2]
    gx, gy = lax.axis_index("gx"), lax.axis_index("gy")
    share = n_well // ny

    barrier = pltpu.get_barrier_semaphore()
    for k in range(1, ny):
        pl.semaphore_signal(barrier, inc=1, device_id={"gy": lax.rem(gy + k, ny)}, device_id_type=MESH)
    for k in range(1, nx):
        pl.semaphore_signal(barrier, inc=1, device_id={"gx": lax.rem(gx + k, nx)}, device_id_type=MESH)

    cells = lambda q, l: (
        press.at[l], sat.at[0, l], sat.at[1, l], direc.at[0, l], direc.at[1, l], direc.at[2, l]
    )[q]
    def split_cells(qs):
        for q in qs:
            need((0, 1, 1, 5, 5, 5)[q])
            for l in range(2):
                high, low = split2(cells(q, l)[...])
                at = (q * 2 + l) * cx
                mhl[at:at + cx, 0:cy] = high.astype(BF16)
                mhl[at:at + cx, cy:2 * cy] = low.astype(BF16)

    def wait_all(landed, sem):
        pltpu.make_async_copy(landed, landed, sem.at[0]).wait()

    def send(src, dst, s_sem, r_sem, where):
        copy = pltpu.make_async_remote_copy(
            src_ref=src, dst_ref=dst, send_sem=s_sem, recv_sem=r_sem, device_id=where, device_id_type=MESH
        )
        copy.start()

    need(8, 9, 6, 15)
    split_cells(range(3))
    all_rows = cy * ny
    shift = all_rows.bit_length() - 1
    first_row = gy * cy

    def split_cell(cell):
        return lax.shift_right_logical(cell, shift), (cell & (all_rows - 1)) - first_row

    def by_product(w, qs):
        cell = jnp.concatenate([perf[w:w + 1, :], perf[w + 1:w + 2, :]], axis=1)
        col, row = split_cell(cell)
        n = cell.shape[1]
        hot = (iota((cy, n), 0) == row).astype(F32).astype(BF16)
        hot = jnp.concatenate([hot, hot], axis=0)
        lines = [jnp.dot(mhl[q * 2 * cx:(q + 1) * 2 * cx, :], hot, preferred_element_type=F32) for q in qs]
        found = [jnp.zeros((8, n), F32)] * len(qs)
        offset = iota((8, n), 0) - col
        for i in range(2 * cx // 8):
            hit = offset == -8 * i
            found = [jnp.where(hit, line[8 * i:8 * i + 8], got) for line, got in zip(lines, found)]
        for q, got in zip(qs, found):
            line = jnp.sum(got, axis=0, keepdims=True)
            gath[q, w:w + 1, :] = line[:, :n // 2]
            gath[q, w + 1:w + 2, :] = line[:, n // 2:]

    def by_lane(w, qs):
        col, row = split_cell(perf[w:w + 1, :])
        n = col.shape[1]
        lanes = jnp.broadcast_to(jnp.clip(row, 0, cy - 1), (8, n))
        offset = jnp.where((row >= 0) & (row < cy), iota((8, n), 0) - col, 1)
        found = [jnp.zeros((8, n), F32)] * len(qs)
        for i in range(2 * cx // 8):
            l, r = divmod(8 * i, cx)
            hit = offset == -8 * i
            for j, q in enumerate(qs):
                line = jnp.take_along_axis(cells(q, l)[r:r + 8, :], lanes, axis=1, mode="promise_in_bounds")
                found[j] = jnp.where(hit, line, found[j])
        for q, got in zip(qs, found):
            gath[q, w:w + 1, :] = jnp.sum(got, axis=0, keepdims=True)

    def gather(qs):
        for w in range(0, n_well - GATHER_BY_LANE, 2):
            by_product(w, qs)
        for w in range(n_well - GATHER_BY_LANE, n_well):
            by_lane(w, qs)

    gather(range(3))
    col, row = split_cell(perf[...])
    weight = jnp.where((row >= 0) & (row < cy), windex[...], 0.0)
    values = [gath[q] for q in range(3)]
    _, _, _, m, _ = mobilities(*values, *values)
    drop = weight * (values[0] - seg_p[...])
    well = iota((n_well, n_well), 0) == iota((n_well, n_well), 1)
    group_col = jnp.sum(jnp.where(well, group[...].astype(F32), 0.0), axis=1, keepdims=True)
    groups = gtarget.shape[1]
    member = group_col == iota((n_well, groups), 1).astype(F32)
    rates = [m[a] * drop for a in range(3)]
    for a in range(3):
        by_well = jnp.sum(rates[a], axis=1, keepdims=True)
        part[a:a + 1, :] = jnp.sum(jnp.where(member, by_well, 0.0), axis=0, keepdims=True)
    pl.semaphore_wait(barrier, nx + ny - 2)
    for k in partners(GY_ORDER, ny):
        to = lax.rem(gy + k, ny)
        send(part.at[pl.ds(0, 3)], rxp.at[k, pl.ds(0, 3)], s_p.at[0], r_p.at[0], {"gy": to})

    need(14, 16, 7)
    guide_col = jnp.sum(jnp.where(well, guide[...], 0.0), axis=1, keepdims=True)
    guide_part = jnp.sum(jnp.where(member, guide_col, 0.0), axis=0, keepdims=True)
    aims[...] = guide_part
    for k in partners(GX_ORDER, nx):
        to = lax.rem(gx + k, nx)
        send(aims, rxg.at[k], s_g.at[0], r_g.at[0], {"gx": to})

    split_cells(range(3, 6))
    gather(range(3, 6))
    slopes = [gath[q] for q in range(3, 6)]
    _, _, _, m, dm = mobilities(*values, *slopes)
    ddrop = weight * (slopes[0] - seg_d[...])
    total = rates[0] + rates[1] + rates[2]
    dtotal = jnp.zeros_like(drop)
    for a in range(3):
        drate = dm[a] * drop + m[a] * ddrop
        gath[a] = rates[a]
        gath[3 + a] = drate
        dtotal = dtotal + drate
    for d in range(ny):
        msg[d, 0:2, :] = total[2 * d:2 * d + 2]
        msg[d, 2:4, :] = dtotal[2 * d:2 * d + 2]
    for k in partners(GY_ORDER, ny):
        to = lax.rem(gy + k, ny)
        send(msg.at[to, pl.ds(0, 4)], rx1.at[k, pl.ds(0, 4)], s_1.at[0], r_1.at[0], {"gy": to})
    need(4)
    lane = iota((cx, cy), 1)
    acc = jnp.zeros((cx, cy), F32)
    for l in range(2):
        for q in range(7):
            block = (
                press.at[l], sat.at[0, l], sat.at[1, l], direc.at[0, l], direc.at[1, l], direc.at[2, l], trans.at[0, l]
            )[q]
            row = 2 * q + l
            halo_tx[0, row:row + 1, :] = block[cx - 1:cx, :]
            halo_tx[1, row:row + 1, :] = block[0:1, :]
            lanes = trans[1, l] if q == 6 else block[...]
            acc = jnp.where(lane == row, lanes[:, cy - 1:cy], acc)
            acc = jnp.where(lane == 16 + row, lanes[:, 0:1], acc)
    flipped = acc.T
    halo_tx[2] = flipped[0:16]
    halo_tx[3] = flipped[16:32]
    halo_tx[0, 14:16, :] = jnp.zeros((2, cy), F32)
    halo_tx[1, 14:16, :] = jnp.zeros((2, cy), F32)
    targets = (
        {"gx": lax.rem(gx + 1, nx)},
        {"gx": lax.rem(gx + nx - 1, nx)},
        {"gy": lax.rem(gy + 1, ny)},
        {"gy": lax.rem(gy + ny - 1, ny)},
    )
    for f in range(4):
        send(halo_tx.at[f], halo_rx.at[f], s_h.at[0], r_h.at[0], targets[f])

    links, reaches = [], []
    need(2, 3, 10)
    n_seg = perf.shape[1]
    def exchange():
        wait_all(rxp.at[pl.ds(1, ny - 1), pl.ds(0, 3)], r_p)
        sums = part[0:3, :]
        for k in range(1, ny):
            sums = sums + rxp[k, 0:3, :]
        msg2[0:3, :] = sums
        for k in partners(GX_ORDER, nx):
            to = lax.rem(gx + k, nx)
            send(msg2.at[pl.ds(0, 3)], rx2.at[k, pl.ds(0, 3)], s_2.at[0], r_2.at[0], {"gx": to})

    weave(
        exchange,
        spread_rates(perf, gath, split_cell, scat, cx, cy),
        cell_terms(press, sat, old, pore, trans, direc, res, jvp, mob, colf),
        descent(parent, gy * share, share, links, reaches),
    )

    wait_all(halo_rx, r_h)
    ins, outs = [], []
    for q in range(7):
        r = slice(2 * q, 2 * q + 2)
        ins.append(jnp.concatenate([halo_rx[0, r], halo_tx[0, r], halo_rx[2, r], halo_tx[2, r]], axis=0))
        outs.append(jnp.concatenate([halo_tx[1, r], halo_rx[1, r], halo_tx[3, r], halo_rx[3, r]], axis=0))
    side = iota((8, cy), 0) // 2
    outer = (
        ((side == 0) & (gx == 0)) | ((side == 1) & (gx == nx - 1))
        | ((side == 2) & (gy == 0)) | ((side == 3) & (gy == ny - 1))
    )
    t = jnp.where(outer, 0.0, ins[6])
    pot, dpot = ins[0] - outs[0], ins[3] - outs[3]
    up, dup = upwinding(pot, dpot)
    m_in, m_out = mobilities(*ins[:6]), mobilities(*outs[:6])
    faces = [
        face(t, pot, dpot, up, dup, m_in[3][a], m_out[3][a], m_in[4][a], m_out[4][a]) for a in range(3)
    ]
    edge[...] = jnp.zeros((cx, cy), F32)
    for a in range(3):
        for o, out in enumerate((res, jvp)):
            for l in range(2):
                out[a, l, 0:1, :] -= faces[a][o][l:l + 1]
                out[a, l, cx - 1:cx, :] += faces[a][o][2 + l:3 + l]
            edge[(2 * a + o) * 4:(2 * a + o) * 4 + 4, :] = faces[a][o][4:8]
    turned = edge[...].T
    for a in range(3):
        for o, out in enumerate((res, jvp)):
            for l in range(2):
                at = (2 * a + o) * 4 + l
                delta = jnp.where(lane == 0, -turned[:, at:at + 1], 0.0)
                delta = jnp.where(lane == cy - 1, turned[:, at + 2:at + 3], delta)
                out[a, l] += delta + scat[a, l * cx:(l + 1) * cx, o * cy:(o + 1) * cy]

    sums = msg[gy, 0:4, :]
    wait_all(rx1.at[pl.ds(1, ny - 1), pl.ds(0, 4)], r_1)
    for k in range(1, ny):
        sums = sums + rx1[k, 0:4, :]

    flows, aboves, owns = [], [], []
    pad = (jnp.zeros((2, n_seg), F32),)
    for i in range(share):
        w = gy * share + i
        vals = jnp.concatenate(split3(sums[i:i + 1]) + split3(sums[2 + i:3 + i]) + pad, axis=0).astype(BF16)
        flow = lax.dot_general(vals, reaches[i], NT, preferred_element_type=F32)
        own = (seg_p[pl.ds(w, 1), :], seg_d[pl.ds(w, 1), :])
        vals = jnp.concatenate(split3(own[0]) + split3(own[1]) + pad, axis=0).astype(BF16)
        above = jnp.dot(vals, links[i], preferred_element_type=F32)
        flows.append((flow[0:1] + flow[1:2] + flow[2:3], flow[3:4] + flow[4:5] + flow[5:6]))
        aboves.append((above[0:1] + above[1:2] + above[2:3], above[3:4] + above[4:5] + above[5:6]))
        owns.append(own)

    need(11, 12, 13)
    wait_all(rxg.at[pl.ds(1, nx - 1)], r_g)
    guide_total = guide_part
    for k in range(1, nx):
        guide_total = guide_total + rxg[k]

    wells = iota((1, n_well), 1)
    segs = iota((1, n_seg), 1)
    names = iota((1, groups), 1).astype(F32)
    for i in range(share):
        w = gy * share + i
        mine = wells == w
        pick = lambda ref: jnp.sum(jnp.where(mine, ref[...].astype(F32), 0.0), axis=1, keepdims=True)
        chosen = names == pick(group)
        named = lambda row: jnp.sum(jnp.where(chosen, row, 0.0), axis=1, keepdims=True)
        target = named(gtarget[...]) * pick(guide) / named(guide_total)
        rated = pick(mode) == 1.0
        (flow, dflow), (above, dabove), (own, down) = flows[i], aboves[i], owns[i]
        inner = own - above - head[pl.ds(w, 1), :] - FRICTION * flow
        root = jnp.where(rated, RATE_SCALE * (flow - target), own - pick(bhp))
        seg_res[i:i + 1, :] = jnp.where(segs == 0, root, inner)
        inner = down - dabove - FRICTION * dflow
        root = jnp.where(rated, RATE_SCALE * dflow, down)
        seg_jvp[i:i + 1, :] = jnp.where(segs == 0, root, inner)

    wait_all(halo_rx, s_h)
    wait_all(rxg.at[pl.ds(1, nx - 1)], s_g)
    wait_all(rxp.at[pl.ds(1, ny - 1), pl.ds(0, 3)], s_p)
    wait_all(rx1.at[pl.ds(1, ny - 1), pl.ds(0, 4)], s_1)
    wait_all(rx2.at[pl.ds(1, nx - 1), pl.ds(0, 3)], s_2)
    everything = msg2[0:3, :]
    wait_all(rx2.at[pl.ds(1, nx - 1), pl.ds(0, 3)], r_2)
    for k in range(1, nx):
        everything = everything + rx2[k, 0:3, :]
    grates[...] = everything


def write_out(*refs):
    copies = [pltpu.make_async_copy(refs[i], refs[5 + i], refs[10].at[i]) for i in range(5)]
    for copy in copies:
        copy.start()
    for copy in copies:
        copy.wait()


def solution(mesh):
    nx, ny = mesh.shape["gx"], mesh.shape["gy"]

    def per_device(
        pressure, saturations, old_mass, pore_volume, transmissibility, direction, seg_pressure, seg_direction,
        perf_cell, well_index, parent, seg_head, well_mode, bhp_limit, guide_rate, group_of, group_target,
    ):
        n_well, n_seg = perf_cell.shape
        _, cx, cy = pressure.shape
        groups = group_target.shape[0]
        vmem = pl.BlockSpec(memory_space=pltpu.VMEM)
        hbm = pl.BlockSpec(memory_space=pltpu.HBM)
        dma = pltpu.SemaphoreType.DMA
        cells = jax.ShapeDtypeStruct(old_mass.shape, F32)
        segs = jax.ShapeDtypeStruct((n_well // ny, n_seg), F32)
        outs = (cells, cells, segs, segs, jax.ShapeDtypeStruct((3, groups), F32))
        row = lambda x: x.reshape(1, -1)
        args = (
            pressure, saturations, old_mass, pore_volume, transmissibility, direction, seg_pressure, seg_direction,
            perf_cell, well_index, parent, seg_head, row(well_mode), row(bhp_limit), row(guide_rate), row(group_of),
            row(group_target),
        )
        made = pl.pallas_call(
            lambda *refs: kernel(nx, ny, *refs),
            out_shape=tuple(pltpu.VMEM(x.shape, x.dtype) for x in outs),
            in_specs=[hbm] * 17,
            out_specs=(vmem,) * 5,
            scratch_shapes=[pltpu.VMEM(x.shape, x.dtype) for x in args] + [
                pltpu.VMEM((12 * cx, 2 * cy), BF16),
                pltpu.VMEM((6, n_well, n_seg), F32),
                pltpu.VMEM((8, 2, cx + 8, cy), F32),
                pltpu.VMEM((6, 2, cx + 8, cy), F32),
                pltpu.VMEM((cx, cy), F32),
                pltpu.VMEM((4, 16, cy), F32),
                pltpu.VMEM((4, 16, cy), F32),
                pltpu.VMEM((ny, 8, n_seg), F32),
                pltpu.VMEM((ny, 8, n_seg), F32),
                pltpu.VMEM((8, groups), F32),
                pltpu.VMEM((nx, 8, groups), F32),
                pltpu.VMEM((8, groups), F32),
                pltpu.VMEM((ny, 8, groups), F32),
                pltpu.VMEM((3, 2 * cx, 2 * cy), F32),
                pltpu.VMEM((1, groups), F32),
                pltpu.VMEM((nx, 1, groups), F32),
                dma((17,)), dma((1,)), dma((1,)), dma((1,)), dma((1,)), dma((1,)), dma((1,)), dma((1,)), dma((1,)), dma((1,)), dma((1,)),
            ],
            compiler_params=pltpu.CompilerParams(
                collective_id=0, has_side_effects=True, vmem_limit_bytes=60 * 1024 * 1024
            ),
            name="newton",
        )(*[pltpu.with_memory_space_constraint(x, pltpu.HBM) for x in args])
        return pl.pallas_call(
            write_out,
            out_shape=outs,
            in_specs=[vmem] * 5,
            out_specs=(hbm,) * 5,
            scratch_shapes=[dma((5,))],
            compiler_params=pltpu.CompilerParams(vmem_limit_bytes=1024 * 1024),
            name="write_out",
        )(*[pltpu.with_memory_space_constraint(x, pltpu.VMEM) for x in made])

    placed = (
        P(None, "gx", "gy"),
        P(None, None, "gx", "gy"),
        P(None, None, "gx", "gy"),
        P(None, "gx", "gy"),
        P(None, None, "gx", "gy"),
        P(None, None, "gx", "gy"),
        P("gx", None),
        P("gx", None),
        P("gx", None),
        P("gx", None),
        P("gx", None),
        P("gx", None),
        P("gx"),
        P("gx"),
        P("gx"),
        P("gx", None),
        P(),
    )
    return jax.shard_map(
        per_device,
        mesh=mesh,
        in_specs=placed,
        out_specs=(
            P(None, None, "gx", "gy"),
            P(None, None, "gx", "gy"),
            P(("gx", "gy"), None),
            P(("gx", "gy"), None),
            P(),
        ),
        check_vma=False,
    )
```

```python
import jax
import jax.numpy as jnp
from jax import lax
from jax.experimental import pallas as pl
from jax.experimental.pallas import tpu as pltpu
from jax.sharding import PartitionSpec as P

COMPRESS = (0.05, 0.2, 1.0)
VISCOSITY = (0.5, 1.0, 0.2)
DENSITY = (1.0, 0.8, 0.2)
ROCK_COMP = 0.01
GRAVITY = 0.05
UPWIND_WIDTH = 0.02
FRICTION = 0.002
RATE_SCALE = 0.1

MESH = pl.DeviceIdType.MESH
F32 = jnp.float32
BF16 = jnp.bfloat16
NT = (((1,), (1,)), ((), ()))

CH = 32
EXCHANGE_AT = 0.45
SPREAD_WELLS = 8
GATHER_BY_LANE = 10
GY_ORDER = (8, 7, 9, 6, 10, 5, 11, 4, 12, 3, 13, 2, 14, 1, 15)
GX_ORDER = (10, 6, 9, 11, 7, 5, 8, 14, 2, 13, 3, 12, 4, 1, 15)
LOAD_ORDER = (8, 0, 1, 9, 6, 15, 5, 7, 14, 16, 4, 2, 3, 10, 11, 12, 13)


def iota(shape, dim):
    return lax.broadcasted_iota(jnp.int32, shape, dim)


def split2(x):
    high = x.astype(BF16).astype(F32)
    return high, x - high


def split3(x):
    high = x.astype(BF16).astype(F32)
    rest = x - high
    mid = rest.astype(BF16).astype(F32)
    return high, mid, rest - mid


def mobilities(press, water, gas, dpress, dwater, dgas):
    satur = (water, 1.0 - water - gas, gas)
    dsatur = (dwater, -dwater - dgas, dgas)
    volumes, mobil, dmobil = [], [], []
    for a in range(3):
        volume = jnp.exp(COMPRESS[a] * (press - 1.0))
        scaled = satur[a] * volume * (1.0 / VISCOSITY[a])
        volumes.append(volume)
        mobil.append(satur[a] * scaled)
        dmobil.append(scaled * (2.0 * dsatur[a] + COMPRESS[a] * satur[a] * dpress))
    return satur, dsatur, volumes, mobil, dmobil


def upwinding(potential, dpotential):
    half = jnp.tanh(potential * (0.5 / UPWIND_WIDTH))
    upwind = 0.5 + 0.5 * half
    dupwind = (1.0 - half * half) * (0.25 / UPWIND_WIDTH) * dpotential
    return upwind, dupwind


def face(trans, pot, dpot, up, dup, m_in, m_out, dm_in, dm_out):
    jump = m_in - m_out
    mean = m_out + up * jump
    dmean = dm_out + up * (dm_in - dm_out) + dup * jump
    flow = trans * pot
    return flow * mean, flow * dmean + (trans * dpot) * mean


def weave(exchange, *strands):
    counts = [n for n, _ in strands]
    places = sorted((((i + 0.5) / n, j) for j, n in enumerate(counts) for i in range(n)))
    for i, (_, j) in enumerate(places):
        if i == round(EXCHANGE_AT * len(places)):
            exchange()
        next(strands[j][1])
    if EXCHANGE_AT == 1:
        exchange()


def spread_rates(perf, gath, split_cell, scat, cx, cy):
    n_well, n_seg = perf.shape

    def pieces():
        for start in range(0, n_well, SPREAD_WELLS):
            hots, hits = [], []
            for w in range(start, start + SPREAD_WELLS):
                col, row = split_cell(perf[w:w + 1, :])
                hot = (iota((2 * cx, n_seg), 0) == col).astype(F32).astype(BF16)
                hots += [hot, hot]
                hit = (iota((cy, n_seg), 0) == row).astype(F32).astype(BF16)
                hits.append(hit.reshape(cy // 16, 16, n_seg))
            hot = jnp.concatenate(hots, axis=1)
            for a in range(3):
                sides = []
                for q in (a, 3 + a):
                    side = []
                    for i in range(SPREAD_WELLS):
                        for part in split2(gath[q, start + i:start + i + 1, :]):
                            wide = jnp.broadcast_to(part, (16, n_seg)).astype(BF16)
                            side.append((hits[i] * wide[None]).reshape(cy, n_seg))
                    sides.append(jnp.concatenate(side, axis=1))
                out = lax.dot_general(hot, jnp.concatenate(sides, axis=0), NT, preferred_element_type=F32)
                if start == 0:
                    scat[a] = out
                else:
                    scat[a] += out
                yield

    return 3 * (n_well // SPREAD_WELLS), pieces()


def descent(parent, first, share, links, reaches):
    n_seg = parent.shape[1]
    levels = (n_seg - 1).bit_length()

    def pieces():
        down = iota((n_seg, n_seg), 0)
        for i in range(share):
            link = down == parent[pl.ds(first + i, 1), :]
            links.append(jnp.where(link, 1.0, 0.0).astype(BF16))
            reach = jnp.where(link | (down == iota((n_seg, n_seg), 1)), 1.0, 0.0).astype(BF16)
            reaches.append(reach)
        for _ in range(levels):
            squares = [jnp.dot(reach, reach, preferred_element_type=F32) for reach in reaches]
            reaches[:] = [jnp.minimum(square, 1.0).astype(BF16) for square in squares]
            yield

    return levels, pieces()


def cell_terms(press, sat, old, pore, trans, direc, res, jvp, mob, colf):
    cx, cy = press.shape[1], press.shape[2]
    steps = cx // CH

    def pieces():
        last = (iota((CH, cy), 1) == cy - 1)
        for l in range(2):
            for q in range(8):
                mob[q, l, cx:cx + 8, :] = jnp.zeros((8, cy), F32)
        colf[:, :, 0:8, :] = jnp.zeros((6, 2, 8, cy), F32)
        for c in range(cx // CH):
            at = slice(c * CH, (c + 1) * CH)
            props = []
            for l in range(2):
                v = (press[l, at], sat[0, l, at], sat[1, l, at], direc[0, l, at], direc[1, l, at], direc[2, l, at])
                satur, dsatur, volume, m, dm = mobilities(*v)
                rock = (1.0 + ROCK_COMP * (v[0] - 1.0)) * pore[l, at]
                drock = ROCK_COMP * v[3] * pore[l, at]
                mob[6, l, at, :] = v[0]
                mob[7, l, at, :] = v[3]
                pot = v[0] - pltpu.roll(v[0], cy - 1, 1)
                dpot = v[3] - pltpu.roll(v[3], cy - 1, 1)
                t = jnp.where(last, 0.0, trans[1, l, at])
                up, dup = upwinding(pot, dpot)
                for a in range(3):
                    mob[a, l, at, :] = m[a]
                    mob[3 + a, l, at, :] = dm[a]
                    mass = satur[a] * volume[a]
                    dmass = (dsatur[a] + COMPRESS[a] * satur[a] * v[3]) * volume[a]
                    f, df = face(
                        t, pot, dpot, up, dup, m[a], pltpu.roll(m[a], cy - 1, 1), dm[a], pltpu.roll(dm[a], cy - 1, 1)
                    )
                    res[a, l, at, :] = rock * mass - old[a, l, at] + (f - pltpu.roll(f, 1, 1))
                    jvp[a, l, at, :] = drock * mass + rock * dmass + (df - pltpu.roll(df, 1, 1))
                props.append((v[0], v[3], m, dm))
            (p0, d0, m0, dm0), (p1, d1, m1, dm1) = props
            t = trans[2, 0, at]
            for a in range(3):
                pot = p0 - p1 + DENSITY[a] * GRAVITY
                dpot = d0 - d1
                up, dup = upwinding(pot, dpot)
                f, df = face(t, pot, dpot, up, dup, m0[a], m1[a], dm0[a], dm1[a])
                res[a, 0, at, :] += f
                jvp[a, 0, at, :] += df
                res[a, 1, at, :] -= f
                jvp[a, 1, at, :] -= df
            yield

        for l in range(2):
            for c in range(cx // CH):
                at = slice(c * CH, (c + 1) * CH)
                nxt = slice(c * CH + 1, (c + 1) * CH + 1)
                here = slice(c * CH + 8, (c + 1) * CH + 8)
                t = trans[0, l, at]
                if c == cx // CH - 1:
                    t = jnp.where(iota((CH, cy), 0) == CH - 1, 0.0, t)
                pot = mob[6, l, at] - mob[6, l, nxt]
                dpot = mob[7, l, at] - mob[7, l, nxt]
                up, dup = upwinding(pot, dpot)
                for a in range(3):
                    f, df = face(
                        t, pot, dpot, up, dup, mob[a, l, at], mob[a, l, nxt], mob[3 + a, l, at], mob[3 + a, l, nxt]
                    )
                    colf[a, l, here, :] = f
                    colf[3 + a, l, here, :] = df
                yield
            for c in range(cx // CH):
                at = slice(c * CH, (c + 1) * CH)
                here = slice(c * CH + 8, (c + 1) * CH + 8)
                prev = slice(c * CH + 7, (c + 1) * CH + 7)
                for a in range(3):
                    res[a, l, at, :] += colf[a, l, here] - colf[a, l, prev]
                    jvp[a, l, at, :] += colf[3 + a, l, here] - colf[3 + a, l, prev]
                yield

    return 5 * steps, pieces()


def partners(order, count):
    return [k for k in order if k < count] if count <= 16 else list(range(1, count))


def kernel(nx, ny, *refs):
    hbm, refs = refs[:17], refs[17:]
    (res, jvp, seg_res, seg_jvp, grates), refs = refs[:5], refs[5:]
    held, refs = refs[:17], refs[17:]
    (
        mhl, gath, mob, colf, edge, halo_tx, halo_rx, msg, rx1, msg2, rx2, part, rxp, scat, aims, rxg,
        s_in, s_h, r_h, s_1, r_1, s_2, r_2, s_p, r_p, s_g, r_g,
    ) = refs
    (
        press, sat, old, pore, trans, direc, seg_p, seg_d, perf, windex, parent, head,
        mode, bhp, guide, group, gtarget,
    ) = held
    loads = [pltpu.make_async_copy(hbm[i], held[i], s_in.at[i]) for i in range(17)]
    for i in LOAD_ORDER:
        if i in (0, 1, 5):
            for j in range(hbm[i].shape[0]):
                pltpu.make_async_copy(hbm[i].at[j], held[i].at[j], s_in.at[i]).start()
        else:
            loads[i].start()
    waited = set()

    def need(*which):
        for i in which:
            if i not in waited:
                waited.add(i)
                loads[i].wait()

    n_well = perf.shape[0]
    cx, cy = press.shape[1], press.shape[2]
    gx, gy = lax.axis_index("gx"), lax.axis_index("gy")
    share = n_well // ny

    barrier = pltpu.get_barrier_semaphore()
    for k in range(1, ny):
        pl.semaphore_signal(barrier, inc=1, device_id={"gy": lax.rem(gy + k, ny)}, device_id_type=MESH)
    for k in range(1, nx):
        pl.semaphore_signal(barrier, inc=1, device_id={"gx": lax.rem(gx + k, nx)}, device_id_type=MESH)

    cells = lambda q, l: (
        press.at[l], sat.at[0, l], sat.at[1, l], direc.at[0, l], direc.at[1, l], direc.at[2, l]
    )[q]
    def split_cells(qs):
        for q in qs:
            need((0, 1, 1, 5, 5, 5)[q])
            for l in range(2):
                high, low = split2(cells(q, l)[...])
                at = (q * 2 + l) * cx
                mhl[at:at + cx, 0:cy] = high.astype(BF16)
                mhl[at:at + cx, cy:2 * cy] = low.astype(BF16)

    def wait_all(landed, sem):
        pltpu.make_async_copy(landed, landed, sem.at[0]).wait()

    def send(src, dst, s_sem, r_sem, where):
        copy = pltpu.make_async_remote_copy(
            src_ref=src, dst_ref=dst, send_sem=s_sem, recv_sem=r_sem, device_id=where, device_id_type=MESH
        )
        copy.start()

    need(8, 9, 6, 15)
    split_cells(range(3))
    all_rows = cy * ny
    shift = all_rows.bit_length() - 1
    first_row = gy * cy

    def split_cell(cell):
        return lax.shift_right_logical(cell, shift), (cell & (all_rows - 1)) - first_row

    def by_product(w, qs):
        cell = jnp.concatenate([perf[w:w + 1, :], perf[w + 1:w + 2, :]], axis=1)
        col, row = split_cell(cell)
        n = cell.shape[1]
        hot = (iota((cy, n), 0) == row).astype(F32).astype(BF16)
        hot = jnp.concatenate([hot, hot], axis=0)
        lines = [jnp.dot(mhl[q * 2 * cx:(q + 1) * 2 * cx, :], hot, preferred_element_type=F32) for q in qs]
        found = [jnp.zeros((8, n), F32)] * len(qs)
        offset = iota((8, n), 0) - col
        for i in range(2 * cx // 8):
            hit = offset == -8 * i
            found = [jnp.where(hit, line[8 * i:8 * i + 8], got) for line, got in zip(lines, found)]
        for q, got in zip(qs, found):
            line = jnp.sum(got, axis=0, keepdims=True)
            gath[q, w:w + 1, :] = line[:, :n // 2]
            gath[q, w + 1:w + 2, :] = line[:, n // 2:]

    def by_lane(w, qs):
        col, row = split_cell(perf[w:w + 1, :])
        n = col.shape[1]
        lanes = jnp.broadcast_to(jnp.clip(row, 0, cy - 1), (8, n))
        offset = jnp.where((row >= 0) & (row < cy), iota((8, n), 0) - col, 1)
        found = [jnp.zeros((8, n), F32)] * len(qs)
        for i in range(2 * cx // 8):
            l, r = divmod(8 * i, cx)
            hit = offset == -8 * i
            for j, q in enumerate(qs):
                line = jnp.take_along_axis(cells(q, l)[r:r + 8, :], lanes, axis=1, mode="promise_in_bounds")
                found[j] = jnp.where(hit, line, found[j])
        for q, got in zip(qs, found):
            gath[q, w:w + 1, :] = jnp.sum(got, axis=0, keepdims=True)

    def gather(qs):
        for w in range(0, n_well - GATHER_BY_LANE, 2):
            by_product(w, qs)
        for w in range(n_well - GATHER_BY_LANE, n_well):
            by_lane(w, qs)

    gather(range(3))
    col, row = split_cell(perf[...])
    weight = jnp.where((row >= 0) & (row < cy), windex[...], 0.0)
    values = [gath[q] for q in range(3)]
    _, _, _, m, _ = mobilities(*values, *values)
    drop = weight * (values[0] - seg_p[...])
    well = iota((n_well, n_well), 0) == iota((n_well, n_well), 1)
    group_col = jnp.sum(jnp.where(well, group[...].astype(F32), 0.0), axis=1, keepdims=True)
    groups = gtarget.shape[1]
    member = group_col == iota((n_well, groups), 1).astype(F32)
    rates = [m[a] * drop for a in range(3)]
    for a in range(3):
        by_well = jnp.sum(rates[a], axis=1, keepdims=True)
        part[a:a + 1, :] = jnp.sum(jnp.where(member, by_well, 0.0), axis=0, keepdims=True)
    pl.semaphore_wait(barrier, nx + ny - 2)
    for k in partners(GY_ORDER, ny):
        to = lax.rem(gy + k, ny)
        send(part.at[pl.ds(0, 3)], rxp.at[k, pl.ds(0, 3)], s_p.at[0], r_p.at[0], {"gy": to})

    need(14, 16, 7)
    guide_col = jnp.sum(jnp.where(well, guide[...], 0.0), axis=1, keepdims=True)
    guide_part = jnp.sum(jnp.where(member, guide_col, 0.0), axis=0, keepdims=True)
    aims[...] = guide_part
    for k in partners(GX_ORDER, nx):
        to = lax.rem(gx + k, nx)
        send(aims, rxg.at[k], s_g.at[0], r_g.at[0], {"gx": to})

    split_cells(range(3, 6))
    gather(range(3, 6))
    slopes = [gath[q] for q in range(3, 6)]
    _, _, _, m, dm = mobilities(*values, *slopes)
    ddrop = weight * (slopes[0] - seg_d[...])
    total = rates[0] + rates[1] + rates[2]
    dtotal = jnp.zeros_like(drop)
    for a in range(3):
        drate = dm[a] * drop + m[a] * ddrop
        gath[a] = rates[a]
        gath[3 + a] = drate
        dtotal = dtotal + drate
    for d in range(ny):
        msg[d, 0:2, :] = total[2 * d:2 * d + 2]
        msg[d, 2:4, :] = dtotal[2 * d:2 * d + 2]
    for k in partners(GY_ORDER, ny):
        to = lax.rem(gy + k, ny)
        send(msg.at[to, pl.ds(0, 4)], rx1.at[k, pl.ds(0, 4)], s_1.at[0], r_1.at[0], {"gy": to})
    need(4)
    lane = iota((cx, cy), 1)
    acc = jnp.zeros((cx, cy), F32)
    for l in range(2):
        for q in range(7):
            block = (
                press.at[l], sat.at[0, l], sat.at[1, l], direc.at[0, l], direc.at[1, l], direc.at[2, l], trans.at[0, l]
            )[q]
            row = 2 * q + l
            halo_tx[0, row:row + 1, :] = block[cx - 1:cx, :]
            halo_tx[1, row:row + 1, :] = block[0:1, :]
            lanes = trans[1, l] if q == 6 else block[...]
            acc = jnp.where(lane == row, lanes[:, cy - 1:cy], acc)
            acc = jnp.where(lane == 16 + row, lanes[:, 0:1], acc)
    flipped = acc.T
    halo_tx[2] = flipped[0:16]
    halo_tx[3] = flipped[16:32]
    halo_tx[0, 14:16, :] = jnp.zeros((2, cy), F32)
    halo_tx[1, 14:16, :] = jnp.zeros((2, cy), F32)
    targets = (
        {"gx": lax.rem(gx + 1, nx)},
        {"gx": lax.rem(gx + nx - 1, nx)},
        {"gy": lax.rem(gy + 1, ny)},
        {"gy": lax.rem(gy + ny - 1, ny)},
    )
    for f in range(4):
        send(halo_tx.at[f], halo_rx.at[f], s_h.at[0], r_h.at[0], targets[f])

    links, reaches = [], []
    need(2, 3, 10)
    n_seg = perf.shape[1]
    def exchange():
        wait_all(rxp.at[pl.ds(1, ny - 1), pl.ds(0, 3)], r_p)
        sums = part[0:3, :]
        for k in range(1, ny):
            sums = sums + rxp[k, 0:3, :]
        msg2[0:3, :] = sums
        for k in partners(GX_ORDER, nx):
            to = lax.rem(gx + k, nx)
            send(msg2.at[pl.ds(0, 3)], rx2.at[k, pl.ds(0, 3)], s_2.at[0], r_2.at[0], {"gx": to})

    weave(
        exchange,
        spread_rates(perf, gath, split_cell, scat, cx, cy),
        cell_terms(press, sat, old, pore, trans, direc, res, jvp, mob, colf),
        descent(parent, gy * share, share, links, reaches),
    )

    wait_all(halo_rx, r_h)
    ins, outs = [], []
    for q in range(7):
        r = slice(2 * q, 2 * q + 2)
        ins.append(jnp.concatenate([halo_rx[0, r], halo_tx[0, r], halo_rx[2, r], halo_tx[2, r]], axis=0))
        outs.append(jnp.concatenate([halo_tx[1, r], halo_rx[1, r], halo_tx[3, r], halo_rx[3, r]], axis=0))
    side = iota((8, cy), 0) // 2
    outer = (
        ((side == 0) & (gx == 0)) | ((side == 1) & (gx == nx - 1))
        | ((side == 2) & (gy == 0)) | ((side == 3) & (gy == ny - 1))
    )
    t = jnp.where(outer, 0.0, ins[6])
    pot, dpot = ins[0] - outs[0], ins[3] - outs[3]
    up, dup = upwinding(pot, dpot)
    m_in, m_out = mobilities(*ins[:6]), mobilities(*outs[:6])
    faces = [
        face(t, pot, dpot, up, dup, m_in[3][a], m_out[3][a], m_in[4][a], m_out[4][a]) for a in range(3)
    ]
    edge[...] = jnp.zeros((cx, cy), F32)
    for a in range(3):
        for o, out in enumerate((res, jvp)):
            for l in range(2):
                out[a, l, 0:1, :] -= faces[a][o][l:l + 1]
                out[a, l, cx - 1:cx, :] += faces[a][o][2 + l:3 + l]
            edge[(2 * a + o) * 4:(2 * a + o) * 4 + 4, :] = faces[a][o][4:8]
    turned = edge[...].T
    for a in range(3):
        for o, out in enumerate((res, jvp)):
            for l in range(2):
                at = (2 * a + o) * 4 + l
                delta = jnp.where(lane == 0, -turned[:, at:at + 1], 0.0)
                delta = jnp.where(lane == cy - 1, turned[:, at + 2:at + 3], delta)
                out[a, l] += delta + scat[a, l * cx:(l + 1) * cx, o * cy:(o + 1) * cy]

    sums = msg[gy, 0:4, :]
    wait_all(rx1.at[pl.ds(1, ny - 1), pl.ds(0, 4)], r_1)
    for k in range(1, ny):
        sums = sums + rx1[k, 0:4, :]

    flows, aboves, owns = [], [], []
    pad = (jnp.zeros((2, n_seg), F32),)
    for i in range(share):
        w = gy * share + i
        vals = jnp.concatenate(split3(sums[i:i + 1]) + split3(sums[2 + i:3 + i]) + pad, axis=0).astype(BF16)
        flow = lax.dot_general(vals, reaches[i], NT, preferred_element_type=F32)
        own = (seg_p[pl.ds(w, 1), :], seg_d[pl.ds(w, 1), :])
        vals = jnp.concatenate(split3(own[0]) + split3(own[1]) + pad, axis=0).astype(BF16)
        above = jnp.dot(vals, links[i], preferred_element_type=F32)
        flows.append((flow[0:1] + flow[1:2] + flow[2:3], flow[3:4] + flow[4:5] + flow[5:6]))
        aboves.append((above[0:1] + above[1:2] + above[2:3], above[3:4] + above[4:5] + above[5:6]))
        owns.append(own)

    need(11, 12, 13)
    wait_all(rxg.at[pl.ds(1, nx - 1)], r_g)
    guide_total = guide_part
    for k in range(1, nx):
        guide_total = guide_total + rxg[k]

    wells = iota((1, n_well), 1)
    segs = iota((1, n_seg), 1)
    names = iota((1, groups), 1).astype(F32)
    for i in range(share):
        w = gy * share + i
        mine = wells == w
        pick = lambda ref: jnp.sum(jnp.where(mine, ref[...].astype(F32), 0.0), axis=1, keepdims=True)
        chosen = names == pick(group)
        named = lambda row: jnp.sum(jnp.where(chosen, row, 0.0), axis=1, keepdims=True)
        target = named(gtarget[...]) * pick(guide) / named(guide_total)
        rated = pick(mode) == 1.0
        (flow, dflow), (above, dabove), (own, down) = flows[i], aboves[i], owns[i]
        inner = own - above - head[pl.ds(w, 1), :] - FRICTION * flow
        root = jnp.where(rated, RATE_SCALE * (flow - target), own - pick(bhp))
        seg_res[i:i + 1, :] = jnp.where(segs == 0, root, inner)
        inner = down - dabove - FRICTION * dflow
        root = jnp.where(rated, RATE_SCALE * dflow, down)
        seg_jvp[i:i + 1, :] = jnp.where(segs == 0, root, inner)

    wait_all(halo_rx, s_h)
    wait_all(rxg.at[pl.ds(1, nx - 1)], s_g)
    wait_all(rxp.at[pl.ds(1, ny - 1), pl.ds(0, 3)], s_p)
    wait_all(rx1.at[pl.ds(1, ny - 1), pl.ds(0, 4)], s_1)
    wait_all(rx2.at[pl.ds(1, nx - 1), pl.ds(0, 3)], s_2)
    everything = msg2[0:3, :]
    wait_all(rx2.at[pl.ds(1, nx - 1), pl.ds(0, 3)], r_2)
    for k in range(1, nx):
        everything = everything + rx2[k, 0:3, :]
    grates[...] = everything


def write_out(*refs):
    copies = [pltpu.make_async_copy(refs[i], refs[5 + i], refs[10].at[i]) for i in range(5)]
    for i, copy in enumerate(copies):
        if i < 2:
            for a in range(refs[i].shape[0]):
                pltpu.make_async_copy(refs[i].at[a], refs[5 + i].at[a], refs[10].at[i]).start()
        else:
            copy.start()
    for copy in copies:
        copy.wait()


def solution(mesh):
    nx, ny = mesh.shape["gx"], mesh.shape["gy"]

    def per_device(
        pressure, saturations, old_mass, pore_volume, transmissibility, direction, seg_pressure, seg_direction,
        perf_cell, well_index, parent, seg_head, well_mode, bhp_limit, guide_rate, group_of, group_target,
    ):
        n_well, n_seg = perf_cell.shape
        _, cx, cy = pressure.shape
        groups = group_target.shape[0]
        vmem = pl.BlockSpec(memory_space=pltpu.VMEM)
        hbm = pl.BlockSpec(memory_space=pltpu.HBM)
        dma = pltpu.SemaphoreType.DMA
        cells = jax.ShapeDtypeStruct(old_mass.shape, F32)
        segs = jax.ShapeDtypeStruct((n_well // ny, n_seg), F32)
        outs = (cells, cells, segs, segs, jax.ShapeDtypeStruct((3, groups), F32))
        row = lambda x: x.reshape(1, -1)
        args = (
            pressure, saturations, old_mass, pore_volume, transmissibility, direction, seg_pressure, seg_direction,
            perf_cell, well_index, parent, seg_head, row(well_mode), row(bhp_limit), row(guide_rate), row(group_of),
            row(group_target),
        )
        made = pl.pallas_call(
            lambda *refs: kernel(nx, ny, *refs),
            out_shape=tuple(pltpu.VMEM(x.shape, x.dtype) for x in outs),
            in_specs=[hbm] * 17,
            out_specs=(vmem,) * 5,
            scratch_shapes=[pltpu.VMEM(x.shape, x.dtype) for x in args] + [
                pltpu.VMEM((12 * cx, 2 * cy), BF16),
                pltpu.VMEM((6, n_well, n_seg), F32),
                pltpu.VMEM((8, 2, cx + 8, cy), F32),
                pltpu.VMEM((6, 2, cx + 8, cy), F32),
                pltpu.VMEM((cx, cy), F32),
                pltpu.VMEM((4, 16, cy), F32),
                pltpu.VMEM((4, 16, cy), F32),
                pltpu.VMEM((ny, 8, n_seg), F32),
                pltpu.VMEM((ny, 8, n_seg), F32),
                pltpu.VMEM((8, groups), F32),
                pltpu.VMEM((nx, 8, groups), F32),
                pltpu.VMEM((8, groups), F32),
                pltpu.VMEM((ny, 8, groups), F32),
                pltpu.VMEM((3, 2 * cx, 2 * cy), F32),
                pltpu.VMEM((1, groups), F32),
                pltpu.VMEM((nx, 1, groups), F32),
                dma((17,)), dma((1,)), dma((1,)), dma((1,)), dma((1,)), dma((1,)), dma((1,)), dma((1,)), dma((1,)), dma((1,)), dma((1,)),
            ],
            compiler_params=pltpu.CompilerParams(
                collective_id=0, has_side_effects=True, vmem_limit_bytes=60 * 1024 * 1024
            ),
            name="newton",
        )(*[pltpu.with_memory_space_constraint(x, pltpu.HBM) for x in args])
        return pl.pallas_call(
            write_out,
            out_shape=outs,
            in_specs=[vmem] * 5,
            out_specs=(hbm,) * 5,
            scratch_shapes=[dma((5,))],
            compiler_params=pltpu.CompilerParams(vmem_limit_bytes=1024 * 1024),
            name="write_out",
        )(*[pltpu.with_memory_space_constraint(x, pltpu.VMEM) for x in made])

    placed = (
        P(None, "gx", "gy"),
        P(None, None, "gx", "gy"),
        P(None, None, "gx", "gy"),
        P(None, "gx", "gy"),
        P(None, None, "gx", "gy"),
        P(None, None, "gx", "gy"),
        P("gx", None),
        P("gx", None),
        P("gx", None),
        P("gx", None),
        P("gx", None),
        P("gx", None),
        P("gx"),
        P("gx"),
        P("gx"),
        P("gx", None),
        P(),
    )
    return jax.shard_map(
        per_device,
        mesh=mesh,
        in_specs=placed,
        out_specs=(
            P(None, None, "gx", "gy"),
            P(None, None, "gx", "gy"),
            P(("gx", "gy"), None),
            P(("gx", "gy"), None),
            P(),
        ),
        check_vma=False,
    )
```
